256 devices in a mesh: row: 8 (over y, x_lo), col: 32 (over x_hi, z, core).
Axes of the slice: x: 4 (x_hi: 2, x_lo: 2; x = x_hi * 2 + x_lo), y: 4, z: 8, core: 2. Of those that a mesh axis runs over, the one named last changes fastest.
Arguments:
- inputs: bfloat16 [1024, 6144], P('col', 'row'), may hold values from -6 to 6
- gain: float32 [6144], P('row'), may hold values from 0.5 to 2
- w_in: bfloat16 [6144, 24576], P('row', 'col'), may hold values from -0.078125 to 0.078125
- bias: float32 [24576], P('col'), may hold values from -3 to 3
- w_out: bfloat16 [24576, 6144], P('col', 'row'), may hold values from -0.078125 to 0.078125
- cotangent: bfloat16 [1024, 6144], P('col', 'row'), may hold values from -6 to 6
Outputs:
- grad_input: bfloat16 [1024, 6144], P('col', 'row')
- grad_w_in: bfloat16 [6144, 24576], P('row', 'col')
- grad_bias: float32 [24576], P('col')
- grad_w_out: bfloat16 [24576, 6144], P('col', 'row')
The draws below stay inside these ranges and needn't reach their ends.
All inputs are finite; a program needn't handle non-finite values.
Results may differ from the reference program's by a relative error of at most 0.023.
Values may be sent and summed in bfloat16 or wider, within the bound.
A program may use at most 64 MiB of HBM per device.

```python
import math
import jax
import jax.numpy as jnp
from jax import lax

D = 6144
FF = 24576
TOKENS = 1024
N_ROW = 8


def level_of(stream_key, shape, pieces, least, high):
    def one(dim, shards_of):
        steps = jax.random.uniform(jax.random.fold_in(jax.random.fold_in(stream_key, 6), dim), (shards_of,), jnp.float32, least / len(pieces), high / len(pieces))
        return jnp.repeat(jnp.exp(steps), shape[dim] // shards_of).reshape((-1,) + (1,) * (len(shape) - dim - 1))

    loudness = one(*pieces[0])
    for cut in pieces[1:]:
        loudness = loudness * one(*cut)
    return loudness


def noise(own_key, shape, deviation, reach, cuts=(), held_as=jnp.bfloat16):
    level = level_of(own_key, shape, cuts, -0.22, 0.18) if cuts else 1.0
    entries = jax.random.normal(own_key, shape, jnp.float32) * deviation * level
    return jnp.minimum(jnp.maximum(entries, -reach), reach).astype(held_as)


def setup_inputs(seed: int = 0) -> dict:
    keys = jax.random.split(jax.random.key(seed), 7)
    return {
        "inputs": noise(keys[0], (TOKENS, D), 1.0, 6.0, ((0, 32), (1, 8))),
        "gain": jnp.clip(jnp.exp(math.log(2.0) - 1.3862944 * jax.random.uniform(keys[1], (D,), jnp.float32) ** level_of(keys[1], (D,), ((0, 8),), -0.2, 0.2)), 0.5, 2.0),
        "w_in": noise(keys[2], (D, FF), D ** -0.5, 0.078125, ((0, 8), (1, 32))),
        "bias": noise(keys[3], (FF,), 0.5, 3.0, ((0, 32),), jnp.float32),
        "w_out": noise(keys[4], (FF, D), D ** -0.5, 0.078125, ((0, 32), (1, 8))),
        "cotangent": noise(keys[5], (TOKENS, D), 1.0, 6.0, ((0, 32), (1, 8))),
    }


def normal_parts(pre_act):
    cumulative = 0.5 * (1.0 + jax.scipy.special.erf(pre_act * 0.7071067811865476))
    density = jnp.exp(-0.5 * pre_act * pre_act) * 0.3989422804014327
    return (cumulative, density)

def blockwise(left, right_rows, count):
    block_len = left.shape[1] // count
    running = jnp.zeros((left.shape[0], right_rows.shape[1]), jnp.float32)
    for index in range(count):
        partial_value = jnp.dot(left[:, index * block_len:(index + 1) * block_len], right_rows[index * block_len:(index + 1) * block_len], preferred_element_type=jnp.float32)
        partial_value = lax.optimization_barrier(partial_value.astype(jnp.bfloat16))
        running = running + partial_value.astype(jnp.float32)
    return running

def reference(inputs, gain, w_in, bias, w_out, cotangent):
    values = inputs.astype(jnp.float32)
    mean_x = lax.optimization_barrier(jnp.mean(values, 1, keepdims=True))
    second = lax.optimization_barrier(jnp.mean(values * values, 1, keepdims=True))
    inv_std = lax.rsqrt(second - mean_x * mean_x + 1e-06)
    centred = (values - mean_x) * inv_std
    normed = (centred * gain).astype(jnp.bfloat16)
    pre_act = blockwise(normed, w_in, N_ROW) + bias
    grad_pre = blockwise(cotangent, w_out.T, N_ROW)
    cumulative, density = normal_parts(pre_act)
    activated = (pre_act * cumulative).astype(jnp.bfloat16)
    grad_hidden = (grad_pre * (cumulative + pre_act * density)).astype(jnp.bfloat16)
    scale = float(TOKENS) ** (-0.5)
    grad_w_out = (jnp.dot(activated.T, cotangent, preferred_element_type=jnp.float32) * scale).astype(jnp.bfloat16)
    grad_w_in = (jnp.dot(normed.T, grad_hidden, preferred_element_type=jnp.float32) * scale).astype(jnp.bfloat16)
    grad_bias = lax.optimization_barrier(jnp.sum(grad_hidden.astype(jnp.float32), 0)) * scale
    grad_normed = jnp.dot(grad_hidden, w_in.T, preferred_element_type=jnp.float32)
    scaled = grad_normed * gain
    first = lax.optimization_barrier(jnp.mean(scaled, 1, keepdims=True))
    crossed = lax.optimization_barrier(jnp.mean(scaled * centred, 1, keepdims=True))
    grad_input = (inv_std * (scaled - first - centred * crossed)).astype(jnp.bfloat16)
    return (grad_input, grad_w_in, grad_bias, grad_w_out)
```

```python
import functools

import jax
import jax.numpy as jnp
from jax import lax
from jax.experimental import pallas as pl
from jax.experimental.pallas import tpu as pltpu
from jax.sharding import PartitionSpec as P

MESH = pl.DeviceIdType.MESH
F32, BF16 = jnp.float32, jnp.bfloat16
D = 6144
EPS = 1e-06
TOKENS, BLK = 1024, 768
CA = 512
CB = BLK - CA
COLS_A, COLS_B = pl.ds(0, CA), pl.ds(CA, CB)
DELTA = (0, 1, -1, 2, -2, 3, -3, 4)
CHUNKS = ((0, 1), (1, 3), (3, 5), (5, 7), (7, 8))
MAX_MSG = 320


def normal_parts(pre_act):
    cumulative = 0.5 * (1.0 + lax.erf(pre_act * 0.7071067811865476))
    density = jnp.exp(-0.5 * pre_act * pre_act) * 0.3989422804014327
    return cumulative, density


def slot_of(delta):
    return DELTA.index(4 if delta in (4, -4) else delta)


def kernel(
    inp, gain, w_in, bias, w_out, cot, gi, gwi, gb, gwo,
    gath, part, ra1, ra2, sa2, rb1, rb2, sb2, hid,
    gk, gs, gr, zs, zr, xs, xr, st, ft, send_sem, recv_sem,
):
    row, col = lax.axis_index("row"), lax.axis_index("col")
    y, xl = row // 2, row % 2
    xh, z, k = col // 16, (col // 2) % 8, col % 2

    def dev(dy=0, dx=0, dh=0, dz=0, dk=0):
        return (
            ((y + dy) % 4) * 2 + (xl + dx) % 2,
            ((xh + dh) % 2) * 16 + ((z + dz) % 8) * 2 + (k + dk) % 2,
        )

    xp = 1 - xl
    ROW_PEERS = [(dy, dx) for dy in range(4) for dx in range(2) if dy or dx]
    partners = [dev(dy=a, dx=b) for a, b in ROW_PEERS]
    partners += [dev(dz=d) for d in range(1, 8)] + [dev(dk=1), dev(dh=1)]
    barrier = pltpu.get_barrier_semaphore()
    for partner in partners:
        pl.semaphore_signal(barrier, inc=1, device_id=partner, device_id_type=MESH)

    sent = {}

    def send(name, src, dst, to):
        index = len(sent)
        copy = pltpu.make_async_remote_copy(
            src_ref=src, dst_ref=dst, send_sem=send_sem.at[index],
            recv_sem=recv_sem.at[index], device_id=to, device_id_type=MESH,
        )
        copy.start()
        sent[name] = copy

    def arrived(name):
        sent[name].wait_recv()

    values = inp[...].astype(F32)
    lane = lax.broadcasted_iota(jnp.int32, (32, 128), 1)

    def pair(a, b):
        return jnp.where(lane < 64, a, b)

    st[0] = pair(
        jnp.sum(values, 1, keepdims=True), jnp.sum(values * values, 1, keepdims=True)
    )
    gath[0, 0:32] = cot[...]
    pl.semaphore_wait(barrier, len(partners))

    def all_row(tag, ref):
        for i, (dy, dx) in enumerate(ROW_PEERS):
            send((tag, i), ref.at[0], ref.at[i + 1], dev(dy=dy, dx=dx))

    def row_sum(tag, ref):
        for i in range(7):
            arrived((tag, i))
        total = ref[0]
        for i in range(1, 8):
            total = total + ref[i]
        return total[:, 0:1] * (1.0 / D), total[:, 64:65] * (1.0 / D)

    def unit(a, slot, u):
        return gath.at[a, pl.ds(slot * 128 + u * 32, 32)]

    def z_first(a, u):
        send(("z", a, u, 2), unit(a, 0, u), unit(a, 2, u), dev(dz=1))
        send(("z", a, u, 1), unit(a, 0, u), unit(a, 1, u), dev(dz=-1))

    def to_sibling(a, slot):
        send(
            ("k", a, slot),
            gath.at[a, pl.ds(slot * 128, 64)],
            gath.at[a, pl.ds(slot * 128 + 64, 64)],
            dev(dk=1),
        )

    def own(a):
        send(("h", a), unit(a, 0, 0), unit(a, 0, 1), dev(dh=1))
        z_first(a, 0)

    def other(a):
        arrived(("h", a))
        z_first(a, 1)
        to_sibling(a, 0)

    def forward_unit(a, u, h):
        if h == 4:
            arrived(("z", a, u, 7))
            return
        right, left = slot_of(-h), slot_of(h)
        arrived(("z", a, u, right))
        if h < 3 or u == 0:
            s = slot_of(-h - 1)
            send(("z", a, u, s), unit(a, right, u), unit(a, s, u), dev(dz=1))
        arrived(("z", a, u, left))
        if h < 3 or u == 1:
            s = slot_of(h + 1)
            send(("z", a, u, s), unit(a, left, u), unit(a, s, u), dev(dz=-1))

    def hop(a, h):
        forward_unit(a, 0, h)
        forward_unit(a, 1, h)
        for slot in (7,) if h == 4 else (slot_of(-h), slot_of(h)):
            to_sibling(a, slot)

    def span(c):
        s0, s1 = CHUNKS[c]
        return s0 * 128, (s1 - s0) * 128

    def at(base, index, size):
        return pl.ds(pl.multiple_of(base + index * size, 16), size)

    def product(a, c):
        off, t = span(c)
        for slot in range(*CHUNKS[c]):
            arrived(("k", a, slot))
        rows = gath[a, off:off + t, :]
        if a == 0:
            out = lax.dot_general(
                rows, w_out[...], (((1,), (1,)), ((), ())), preferred_element_type=F32
            )
        else:
            out = jnp.dot(rows, w_in[...], preferred_element_type=F32)
        part[a, off:off + t, :] = out.astype(BF16)
        send(
            ("a1", a, c),
            part.at[a, at(off, xp, t // 2), COLS_A],
            ra1.at[a, pl.ds(off // 2, t // 2)],
            dev(dx=1),
        )
        for dy in (1, 3, 2):
            send(
                ("b1", a, c, dy),
                part.at[a, at(off, (y + dy) % 4, t // 4), COLS_B],
                rb1.at[a, dy - 1, pl.ds(off // 4, t // 4)],
                dev(dy=dy),
            )

    def reduce2(a, c):
        off, t = span(c)
        o2, o4, o8, t2, t4, t8 = off // 2, off // 4, off // 8, t // 2, t // 4, t // 8
        arrived(("a1", a, c))
        total = part[a, at(off, xl, t2), COLS_A].astype(F32) + ra1[a, o2:o2 + t2].astype(F32)
        sa2[a, o2:o2 + t2] = total.astype(BF16)
        for dy in (1, 3, 2):
            send(
                ("a2", a, c, dy),
                sa2.at[a, at(o2, (y + dy) % 4, t8)],
                ra2.at[a, dy - 1, pl.ds(o8, t8)],
                dev(dy=dy),
            )
        total = part[a, at(off, y, t4), COLS_B].astype(F32)
        for dy in (1, 3, 2):
            arrived(("b1", a, c, dy))
            total = total + rb1[a, dy - 1, o4:o4 + t4].astype(F32)
        sb2[a, o4:o4 + t4] = total.astype(BF16)
        send(("b2", a, c), sb2.at[a, at(o4, xp, t8)], rb2.at[a, pl.ds(o8, t8)], dev(dx=1))

    def rows_a(c):
        off, t = span(c)
        return at(off, xl * 4 + y, t // 8)

    def rows_b(c):
        off, t = span(c)
        return at(off, y * 2 + xl, t // 8)

    def elementwise(c):
        off, t = span(c)
        o2, o4, o8, t8 = off // 2, off // 4, off // 8, t // 8

        def finish(rows, cols, bias_part, totals):
            pre_act = totals[1] + bias_part
            cumulative, density = normal_parts(pre_act)
            hid[0, rows, cols] = (totals[0] * (cumulative + pre_act * density)).astype(BF16)
            hid[1, rows, cols] = (pre_act * cumulative).astype(BF16)

        totals = []
        for a in (0, 1):
            total = sa2[a, at(o2, y, t8)].astype(F32)
            for dy in (1, 3, 2):
                arrived(("a2", a, c, dy))
                total = total + ra2[a, dy - 1, o8:o8 + t8].astype(F32)
            totals.append(total)
        finish(rows_a(c), COLS_A, bias[:, 0:CA], totals)
        totals = []
        for a in (0, 1):
            arrived(("b2", a, c))
            totals.append(sb2[a, at(o4, xl, t8)].astype(F32) + rb2[a, o8:o8 + t8].astype(F32))
        finish(rows_b(c), COLS_B, bias[:, CA:BLK], totals)

    def gather1(g, c):
        part_a = hid.at[g, rows_a(c), COLS_A]
        for dy in (1, 3, 2):
            send(("g1", g, c, dy), part_a, part_a, dev(dy=dy))
        part_b = hid.at[g, rows_b(c), COLS_B]
        send(("h1", g, c), part_b, part_b, dev(dx=1))

    def gather2(g, c):
        off, t = span(c)
        for dy in (1, 3, 2):
            arrived(("g1", g, c, dy))
        part_a = hid.at[g, at(off, xl, t // 2), COLS_A]
        send(("g2", g, c), part_a, part_a, dev(dx=1))
        arrived(("h1", g, c))
        part_b = hid.at[g, at(off, y, t // 4), COLS_B]
        for dy in (1, 3, 2):
            send(("h2", g, c, dy), part_b, part_b, dev(dy=dy))

    def gathered(g, c):
        arrived(("g2", g, c))
        for dy in (1, 3, 2):
            arrived(("h2", g, c, dy))

    def back_product(c):
        gathered(0, c)
        off, t = span(c)
        s0, s1 = CHUNKS[c]
        out = lax.dot_general(
            hid[0, off:off + t, :], w_in[...], (((1,), (1,)), ((), ())),
            preferred_element_type=F32,
        )
        for slot in range(s0, s1):
            base = (slot - s0) * 128
            gk[slot] = out[base:base + 64]
            gs[slot] = out[base + 64:base + 128].astype(BF16)
        send(("n", c), gs.at[pl.ds(s0, s1 - s0)], gr.at[pl.ds(s0, s1 - s0)], dev(dk=1))

    def scatter_z(c):
        arrived(("n", c))
        for slot in range(*CHUNKS[c]):
            total = gk[slot] + gr[slot].astype(F32)
            if slot == 0:
                gk[0] = total
            else:
                zs[slot] = total.astype(BF16)
                send(("s", slot), zs.at[slot], zr.at[slot], dev(dz=DELTA[slot]))

    own(0)
    all_row("st", st)
    other(0)
    mean_x, second = row_sum("st", st)
    inv_std = lax.rsqrt(second - mean_x * mean_x + EPS)
    centred = (values - mean_x) * inv_std
    gath[1, 0:32] = (centred * gain[...]).astype(BF16)
    own(1)
    product(0, 0)
    other(1)
    hop(0, 1)
    product(1, 0)
    hop(1, 1)
    product(0, 1)
    reduce2(0, 0)
    hop(0, 2)
    product(1, 1)
    reduce2(1, 0)
    hop(1, 2)
    product(0, 2)
    reduce2(0, 1)
    hop(0, 3)
    product(1, 2)
    reduce2(1, 1)
    hop(1, 3)
    product(0, 3)
    reduce2(0, 2)
    hop(0, 4)
    elementwise(1)
    gather1(0, 1)
    product(1, 3)
    reduce2(1, 2)
    hop(1, 4)
    product(0, 4)
    reduce2(0, 3)
    elementwise(2)
    gather1(0, 2)
    product(1, 4)
    reduce2(1, 3)
    gather2(0, 1)
    elementwise(3)
    gather1(0, 3)
    gather1(1, 1)
    reduce2(0, 4)
    reduce2(1, 4)
    gather2(0, 2)
    elementwise(4)
    gather1(0, 4)
    gather1(1, 2)
    back_product(1)
    gather2(0, 3)
    elementwise(0)
    gather1(0, 0)
    gather1(1, 3)
    scatter_z(1)
    back_product(2)
    gather2(0, 4)
    gather1(1, 4)
    gather1(1, 0)
    scatter_z(2)
    gather2(0, 0)
    gather2(1, 1)
    back_product(3)
    gather2(1, 2)
    scatter_z(3)
    back_product(4)
    gather2(1, 3)
    scatter_z(4)
    back_product(0)
    gather2(1, 4)
    gather2(1, 0)
    scatter_z(0)

    scale = float(TOKENS) ** (-0.5)

    def outer(left, right, out):
        for i in range(3):
            out[i * 256:(i + 1) * 256, :] = (
                lax.dot_general(
                    left[:, i * 256:(i + 1) * 256], right, (((0,), (0,)), ((), ())),
                    preferred_element_type=F32,
                )
                * scale
            ).astype(BF16)

    total = gk[0]
    for slot in range(1, 8):
        arrived(("s", slot))
        total = total + zr[slot].astype(F32)
    xs[...] = total[32:64].astype(BF16)
    send("x", xs, xr, dev(dh=1))
    outer(gath.at[1], hid[0], gwi)
    arrived("x")
    scaled = (total[0:32] + xr[...].astype(F32)) * gain[...]
    ft[0] = pair(
        jnp.sum(scaled, 1, keepdims=True), jnp.sum(scaled * centred, 1, keepdims=True)
    )
    all_row("ft", ft)
    gb[...] = jnp.sum(hid[0].astype(F32), 0, keepdims=True) * scale
    first, cross = row_sum("ft", ft)
    gi[...] = (inv_std * (scaled - first - centred * cross)).astype(BF16)
    for c in range(5):
        gathered(1, c)
    outer(hid.at[1], gath[0], gwo)
    for copy in sent.values():
        copy.wait_send()


def local(inputs, gain, w_in, bias, w_out, cotangent):
    vmem = pl.BlockSpec(memory_space=pltpu.VMEM)
    grad_input, grad_w_in, grad_bias, grad_w_out = pl.pallas_call(
        kernel,
        out_shape=(
            jax.ShapeDtypeStruct((32, BLK), BF16),
            jax.ShapeDtypeStruct((BLK, BLK), BF16),
            jax.ShapeDtypeStruct((1, BLK), F32),
            jax.ShapeDtypeStruct((BLK, BLK), BF16),
        ),
        in_specs=[vmem] * 6,
        out_specs=[vmem] * 4,
        scratch_shapes=[
            pltpu.VMEM((2, TOKENS, BLK), BF16),
            pltpu.VMEM((2, TOKENS, BLK), BF16),
            pltpu.VMEM((2, TOKENS // 2, CA), BF16),
            pltpu.VMEM((2, 3, TOKENS // 8, CA), BF16),
            pltpu.VMEM((2, TOKENS // 2, CA), BF16),
            pltpu.VMEM((2, 3, TOKENS // 4, CB), BF16),
            pltpu.VMEM((2, TOKENS // 8, CB), BF16),
            pltpu.VMEM((2, TOKENS // 4, CB), BF16),
            pltpu.VMEM((2, TOKENS, BLK), BF16),
            pltpu.VMEM((8, 64, BLK), F32),
            pltpu.VMEM((8, 64, BLK), BF16),
            pltpu.VMEM((8, 64, BLK), BF16),
            pltpu.VMEM((8, 64, BLK), BF16),
            pltpu.VMEM((8, 64, BLK), BF16),
            pltpu.VMEM((32, BLK), BF16),
            pltpu.VMEM((32, BLK), BF16),
            pltpu.VMEM((8, 32, 128), F32),
            pltpu.VMEM((8, 32, 128), F32),
            pltpu.SemaphoreType.DMA((MAX_MSG,)),
            pltpu.SemaphoreType.DMA((MAX_MSG,)),
        ],
        compiler_params=pltpu.CompilerParams(
            collective_id=0, has_side_effects=True, vmem_limit_bytes=48 * 2**20
        ),
        name="mlp_backward",
    )(inputs, gain.reshape(1, BLK), w_in, bias.reshape(1, BLK), w_out, cotangent)
    return grad_input, grad_w_in, grad_bias.reshape(BLK), grad_w_out


def solution(mesh):
    in_specs = (
        P("col", "row"),
        P("row"),
        P("row", "col"),
        P("col"),
        P("col", "row"),
        P("col", "row"),
    )
    out_specs = (P("col", "row"), P("row", "col"), P("col"), P("col", "row"))
    return jax.shard_map(local, mesh=mesh, in_specs=in_specs, out_specs=out_specs, check_vma=False)
```

```python
import functools

import jax
import jax.numpy as jnp
from jax import lax
from jax.experimental import pallas as pl
from jax.experimental.pallas import tpu as pltpu
from jax.sharding import PartitionSpec as P

MESH = pl.DeviceIdType.MESH
F32, BF16 = jnp.float32, jnp.bfloat16
D = 6144
EPS = 1e-06
TOKENS, BLK = 1024, 768
CA = 256
CB = BLK - CA
HA, HB = CA // 2, CB // 2
COLS_A, COLS_B = pl.ds(0, CA), pl.ds(CA, CB)
DELTA = (0, 1, -1, 2, -2, 3, -3, 4)
CHUNKS = ((0, 1), (1, 3), (3, 5), (5, 7), (7, 8))
N_SEND, N_RECV = 40, 200


def normal_parts(pre_act):
    cumulative = 0.5 * (1.0 + lax.erf(pre_act * 0.7071067811865476))
    density = jnp.exp(-0.5 * pre_act * pre_act) * 0.3989422804014327
    return cumulative, density


def slot_of(delta):
    return DELTA.index(4 if delta in (4, -4) else delta)


def kernel(
    inp_hbm, gain_hbm, w_in_hbm, bias_hbm, w_out_hbm, cot_hbm, gi, gwi, gb, gwo,
    inp, gain, w_in, bias, w_out, gath, part, ra1, sa, raf, ra3, rbf, rb, sb, rbx, hid,
    gk, gs, gr, xs, xr, zs, zr, acc, st, ft, load_sem, send_sem, recv_sem,
):
    row, col = lax.axis_index("row"), lax.axis_index("col")
    y, xl = row // 2, row % 2
    xh, z, k = col // 16, (col // 2) % 8, col % 2

    def dev(dy=0, dx=0, dh=0, dz=0, dk=0):
        return (
            ((y + dy + 4) % 4) * 2 + (xl + dx) % 2,
            ((xh + dh) % 2) * 16 + ((z + dz + 8) % 8) * 2 + (k + dk) % 2,
        )

    xp, yp, ym, y2 = 1 - xl, (y + 1) % 4, (y + 3) % 4, (y + 2) % 4
    ROW_PEERS = [(dy, dx) for dy in range(4) for dx in range(2) if dy or dx]
    partners = [dev(dy=a, dx=b) for a, b in ROW_PEERS]
    partners += [dev(dz=1), dev(dz=-1), dev(dk=1), dev(dh=1), dev(dh=1, dk=1)]
    barrier = pltpu.get_barrier_semaphore()
    for partner in partners:
        pl.semaphore_signal(barrier, inc=1, device_id=partner, device_id_type=MESH)
    loads = [
        pltpu.make_async_copy(src, dst, load_sem.at[i])
        for i, (src, dst) in enumerate((
            (cot_hbm, gath.at[0, 0, 0, pl.ds(0, 32)]),
            (inp_hbm, inp),
            (gain_hbm, gain.at[0]),
            (bias_hbm, bias.at[0]),
            (w_out_hbm, w_out),
            (w_in_hbm, w_in),
        ))
    ]
    for load in loads:
        load.start()

    send_index, recv_index = {}, {}

    def send(key, kind, src, dst, to):
        pltpu.make_async_remote_copy(
            src_ref=src, dst_ref=dst,
            send_sem=send_sem.at[send_index.setdefault(kind, len(send_index))],
            recv_sem=recv_sem.at[recv_index.setdefault(key, len(recv_index))],
            device_id=to, device_id_type=MESH,
        ).start()

    def all_of(ref, kind, key):
        return pltpu.make_async_remote_copy(
            src_ref=ref, dst_ref=ref, send_sem=send_sem.at[send_index[kind]],
            recv_sem=recv_sem.at[recv_index[key]], device_id=dev(dk=1), device_id_type=MESH,
        )

    def arrived(key, ref):
        all_of(ref, ("st",), key).wait_recv()

    def departed(kind, ref):
        all_of(ref, kind, ("st",)).wait_send()

    lane = lax.broadcasted_iota(jnp.int32, (32, 128), 1)

    def pair(a, b):
        return jnp.where(lane < 64, a, b)

    loads[0].wait()
    loads[1].wait()
    values = inp[...].astype(F32)
    st[0] = pair(
        jnp.sum(values, 1, keepdims=True), jnp.sum(values * values, 1, keepdims=True)
    )
    pl.semaphore_wait(barrier, len(partners))

    def all_row(tag, ref):
        for i, (dy, dx) in enumerate(ROW_PEERS):
            send((tag,), (tag,), ref.at[0], ref.at[i + 1], dev(dy=dy, dx=dx))

    def row_sum(tag, ref):
        arrived((tag,), ref.at[pl.ds(1, 7)])
        total = ref[0]
        for i in range(1, 8):
            total = total + ref[i]
        return total[:, 0:1] * (1.0 / D), total[:, 64:65] * (1.0 / D)

    def unit(a, slot, u):
        return gath.at[a, slot, 0, pl.ds(u * 32, 32)]

    def pass_z(a, u, origin, slot, dz):
        send(("z", a, u, slot), ("z", a), unit(a, origin, u), unit(a, slot, u), dev(dz=dz))

    def z_first(a, u):
        pass_z(a, u, 0, 2, 1)
        pass_z(a, u, 0, 1, -1)

    def to_sibling(a, c, slot, u):
        mine = unit(a, slot, u)
        send(("k", a, c), ("k", a), mine, gath.at[a, slot, 1, pl.ds(u * 32, 32)], dev(dk=1))

    def own(a):
        mine = unit(a, 0, 0)
        send(("h", a), ("o", a), mine, unit(a, 0, 1), dev(dh=1))
        z_first(a, 0)
        send(("k", a, 0), ("o", a), mine, gath.at[a, 0, 1, pl.ds(32, 32)], dev(dh=1, dk=1))
        send(("k", a, 0), ("o", a), mine, gath.at[a, 0, 1, pl.ds(0, 32)], dev(dk=1))

    def other(a):
        arrived(("h", a), unit(a, 0, 1))
        z_first(a, 1)

    def hop(a, u, h):
        if h == 4:
            arrived(("z", a, u, 7), unit(a, 7, u))
            to_sibling(a, h, 7, u)
            return
        for slot, dz in ((slot_of(-h), 1), (slot_of(h), -1)):
            arrived(("z", a, u, slot), unit(a, slot, u))
            if h < 3 or u == (dz < 0):
                pass_z(a, u, slot, slot_of(-dz * (h + 1)), dz)
            to_sibling(a, h, slot, u)

    def span(c):
        s0, s1 = CHUNKS[c]
        return s0 * 128, (s1 - s0) * 128

    def at(base, index, size):
        return pl.ds(pl.multiple_of(base + index * size, 16), size)

    def product(a, c):
        off, t = span(c)
        s0, s1 = CHUNKS[c]
        arrived(("k", a, c), gath.at[a, pl.ds(s0, s1 - s0), 1])
        rows = gath[a, s0:s1].reshape(t, BLK)
        if a == 0:
            out = lax.dot_general(
                rows, w_out[...], (((1,), (1,)), ((), ())), preferred_element_type=F32
            )
        else:
            out = jnp.dot(rows, w_in[...], preferred_element_type=F32)
        part[a, off:off + t, :] = out.astype(BF16)
        far = at(off, y2, t // 4)
        quarter = pl.ds(off // 4, t // 4)
        for i, dy in ((0, 1), (1, -1)):
            send(
                ("bf", a, c), ("p", a), part.at[a, far, pl.ds(CA + i * HB, HB)],
                rbf.at[a, i, quarter], dev(dy=dy),
            )
        send(
            ("a1", a, c), ("p", a), part.at[a, at(off, xp, t // 2), COLS_A],
            ra1.at[a, pl.ds(off // 2, t // 2)], dev(dx=1),
        )

    def merge(ref, a, rows, cols, other):
        ref[a, rows, cols] = (ref[a, rows, cols].astype(F32) + other.astype(F32)).astype(BF16)

    def reduce2(a, c):
        off, t = span(c)
        o2, o4, o8, t2, t4, t8 = off // 2, off // 4, off // 8, t // 2, t // 4, t // 8
        arrived(("bf", a, c), rbf.at[a, :, pl.ds(o4, t4)])
        for i, block, start, dy in ((0, yp, CA, 1), (1, ym, CA + HB, -1)):
            merge(part, a, at(off, block, t4), pl.ds(start, HB), rbf[a, i, o4:o4 + t4])
            send(
                ("b", a, c), ("b", a), part.at[a, at(off, block, t4), COLS_B],
                rb.at[a, i, pl.ds(o4, t4)], dev(dy=dy),
            )
        arrived(("a1", a, c), ra1.at[a, pl.ds(o2, t2)])
        total = part[a, at(off, xl, t2), COLS_A].astype(F32) + ra1[a, o2:o2 + t2].astype(F32)
        sa[a, o2:o2 + t2] = total.astype(BF16)
        for i, dy in ((0, 1), (1, -1)):
            send(
                ("af", a, c), ("af", a), sa.at[a, at(o2, y2, t8), pl.ds(i * HA, HA)],
                raf.at[a, i, pl.ds(o8, t8)], dev(dy=dy),
            )

    def reduce3(a, c):
        off, t = span(c)
        o2, o4, o8, t4, t8 = off // 2, off // 4, off // 8, t // 4, t // 8
        arrived(("af", a, c), raf.at[a, :, pl.ds(o8, t8)])
        for i, block, start, dy in ((0, yp, 0, 1), (1, ym, HA, -1)):
            merge(sa, a, at(o2, block, t8), pl.ds(start, HA), raf[a, i, o8:o8 + t8])
            send(
                ("a3", a, c), ("a3", a), sa.at[a, at(o2, block, t8)],
                ra3.at[a, i, pl.ds(o8, t8)], dev(dy=dy),
            )
        arrived(("b", a, c), rb.at[a, :, pl.ds(o4, t4)])
        total = part[a, at(off, y, t4), COLS_B].astype(F32)
        for i in (0, 1):
            total = total + rb[a, i, o4:o4 + t4].astype(F32)
        sb[a, o4:o4 + t4] = total.astype(BF16)
        send(
            ("b3", a, c), ("b3", a), sb.at[a, at(o4, xp, t8)], rbx.at[a, pl.ds(o8, t8)],
            dev(dx=1),
        )

    def rows_a(c):
        off, t = span(c)
        return at(off, xl * 4 + y, t // 8)

    def rows_b(c):
        off, t = span(c)
        return at(off, y * 2 + xl, t // 8)

    def elementwise(c):
        off, t = span(c)
        o2, o4, o8, t8 = off // 2, off // 4, off // 8, t // 8

        def finish(rows, cols, bias_part, totals):
            pre_act = totals[1] + bias_part
            cumulative, density = normal_parts(pre_act)
            hid[0, rows, cols] = (totals[0] * (cumulative + pre_act * density)).astype(BF16)
            hid[1, rows, cols] = (pre_act * cumulative).astype(BF16)

        totals = []
        for a in (0, 1):
            arrived(("a3", a, c), ra3.at[a, :, pl.ds(o8, t8)])
            total = sa[a, at(o2, y, t8)].astype(F32)
            for i in (0, 1):
                total = total + ra3[a, i, o8:o8 + t8].astype(F32)
            totals.append(total)
        finish(rows_a(c), COLS_A, bias[:, 0:CA], totals)
        totals = []
        for a in (0, 1):
            arrived(("b3", a, c), rbx.at[a, pl.ds(o8, t8)])
            totals.append(sb[a, at(o4, xl, t8)].astype(F32) + rbx[a, o8:o8 + t8].astype(F32))
        finish(rows_b(c), COLS_B, bias[:, CA:BLK], totals)

    def share(key, kind, ref, to):
        send(key, kind, ref, ref, to)

    def block_a(g, c, index, cols=COLS_A):
        off, t = span(c)
        return hid.at[g, at(off, xl * 4 + index, t // 8), cols]

    def block_b(g, c, index, cols=COLS_B):
        off, t = span(c)
        return hid.at[g, at(off, index, t // 4), cols]

    def gather1(g, c):
        share(("h1", g, c), ("g1", g), hid.at[g, rows_b(c), COLS_B], dev(dx=1))
        for i, dy in ((0, 1), (1, -1)):
            share(("g1", g, c, i), ("g1", g), block_a(g, c, y), dev(dy=dy))

    def gather2(g, c):
        off, t = span(c)
        arrived(("h1", g, c), hid.at[g, at(off, y * 2 + xp, t // 8), COLS_B])
        for i, dy in ((0, 1), (1, -1)):
            share(("h2", g, c, i), ("h2", g), block_b(g, c, y), dev(dy=dy))
        for i, block, dy in ((0, ym, 1), (1, yp, -1)):
            arrived(("g1", g, c, i), block_a(g, c, block))
            share(("g2", g, c), ("g2", g), block_a(g, c, block, pl.ds(i * HA, HA)), dev(dy=dy))

    def gather3(g, c):
        off, t = span(c)
        for i, block, dy in ((0, ym, 1), (1, yp, -1)):
            arrived(("h2", g, c, i), block_b(g, c, block))
            share(("h3", g, c), ("g3", g), block_b(g, c, block, pl.ds(CA + i * HB, HB)), dev(dy=dy))
        arrived(("g2", g, c), block_a(g, c, y2))
        share(("g3", g, c), ("g3", g), hid.at[g, at(off, xl, t // 2), COLS_A], dev(dx=1))

    def gathered(g, c):
        off, t = span(c)
        arrived(("g3", g, c), hid.at[g, at(off, xp, t // 2), COLS_A])
        arrived(("h3", g, c), block_b(g, c, y2))

    def back_product(c):
        gathered(0, c)
        off, t = span(c)
        s0, s1 = CHUNKS[c]
        out = lax.dot_general(
            hid[0, off:off + t, :], w_in[...], (((1,), (1,)), ((), ())),
            preferred_element_type=F32,
        )
        for slot in range(s0, s1):
            base = (slot - s0) * 128
            gk[slot] = out[base:base + 64]
            gs[slot] = out[base + 64:base + 128].astype(BF16)
        send(("n", c), ("n",), gs.at[pl.ds(s0, s1 - s0)], gr.at[pl.ds(s0, s1 - s0)], dev(dk=1))

    def scatter_x(c):
        s0, s1 = CHUNKS[c]
        arrived(("n", c), gr.at[pl.ds(s0, s1 - s0)])
        for slot in range(s0, s1):
            total = gk[slot] + gr[slot].astype(F32)
            gk[slot, 0:32] = total[0:32]
            xs[slot] = total[32:64].astype(BF16)
        send(("x", c), ("x",), xs.at[pl.ds(s0, s1 - s0)], xr.at[pl.ds(s0, s1 - s0)], dev(dh=1))

    def scatter_z(c):
        s0, s1 = CHUNKS[c]
        arrived(("x", c), xr.at[pl.ds(s0, s1 - s0)])
        for slot in range(s0, s1):
            total = gk[slot, 0:32] + xr[slot].astype(F32)
            if slot == 0:
                gk[0, 0:32] = total
            else:
                zs[slot] = total.astype(BF16)
                send(("s",), ("s",), zs.at[slot], zr.at[slot], dev(dz=DELTA[slot]))

    scale = float(TOKENS) ** (-0.5)
    tiles = [(i * 256, (i + 1) * 256) for i in range(3)]

    def outer(left, right):
        return lax.dot_general(
            left, right, (((0,), (0,)), ((), ())), preferred_element_type=F32
        )

    def flat(a, s0=0, s1=8):
        return gath[a, s0:s1].reshape((s1 - s0) * 128, BLK)

    def grad_in():
        for i, j in tiles:
            gwi[i:j, :] = (outer(flat(1)[:, i:j], hid[0]) * scale).astype(BF16)
        gb[...] = (jnp.sum(hid[0].astype(F32), 0, keepdims=True) * scale).reshape(BLK)

    def total_back():
        total = gk[0, 0:32]
        arrived(("s",), zr.at[pl.ds(1, 7)])
        for slot in range(1, 8):
            total = total + zr[slot].astype(F32)
        scaled = total * gain[...]
        ft[0] = pair(
            jnp.sum(scaled, 1, keepdims=True), jnp.sum(scaled * centred, 1, keepdims=True)
        )
        all_row("ft", ft)
        return scaled

    def finish_input(scaled):
        first, cross = row_sum("ft", ft)
        gi[...] = (inv_std * (scaled - first - centred * cross)).astype(BF16)

    def partial_out():
        for c in range(4):
            gathered(1, c)
        for i, j in tiles:
            acc[i:j, :] = outer(hid[1, 0:896, i:j], flat(0, 0, 7))

    def last_out():
        gathered(1, 4)
        for i, j in tiles:
            gwo[i:j, :] = (
                (acc[i:j, :] + outer(hid[1, 896:TOKENS, i:j], flat(0, 7, 8))) * scale
            ).astype(BF16)

    own(0)
    all_row("st", st)
    mean_x, second = row_sum("st", st)
    inv_std = lax.rsqrt(second - mean_x * mean_x + EPS)
    centred = (values - mean_x) * inv_std
    loads[2].wait()
    gath[1, 0, 0, 0:32] = (centred * gain[...]).astype(BF16)
    own(1)
    other(0)
    hop(0, 0, 1)
    loads[4].wait()
    product(0, 0)
    other(1)
    loads[5].wait()
    product(1, 0)
    hop(0, 1, 1)
    hop(1, 0, 1)
    reduce2(0, 0)
    product(0, 1)
    hop(1, 1, 1)
    hop(0, 0, 2)
    reduce2(1, 0)
    hop(0, 1, 2)
    product(1, 1)
    reduce3(0, 0)
    product(0, 2)
    hop(1, 0, 2)
    reduce2(0, 1)
    hop(1, 1, 2)
    reduce3(1, 0)
    hop(0, 0, 3)
    product(1, 2)
    reduce2(1, 1)
    hop(0, 1, 3)
    reduce2(0, 2)
    reduce3(0, 1)
    product(0, 3)
    hop(1, 1, 3)
    hop(1, 0, 3)
    hop(0, 0, 4)
    reduce2(1, 2)
    hop(0, 1, 4)
    product(1, 3)
    reduce3(1, 1)
    hop(1, 1, 4)
    hop(1, 0, 4)
    product(0, 4)
    reduce2(0, 3)
    product(1, 4)
    reduce3(1, 2)
    reduce3(0, 2)
    loads[3].wait()
    elementwise(0)
    reduce2(0, 4)
    elementwise(1)
    gather1(0, 1)
    reduce2(1, 3)
    elementwise(2)
    gather1(0, 2)
    reduce2(1, 4)
    gather2(0, 1)
    gather1(0, 0)
    reduce3(1, 3)
    reduce3(0, 3)
    reduce3(1, 4)
    reduce3(0, 4)
    gather2(0, 2)
    gather3(0, 1)
    elementwise(3)
    gather1(0, 3)
    elementwise(4)
    gather2(0, 0)
    gather1(0, 4)
    gather1(1, 0)
    gather1(1, 2)
    gather3(0, 2)
    gather2(0, 3)
    gather2(0, 4)
    gather3(0, 0)
    gather1(1, 3)
    gather1(1, 1)
    back_product(1)
    gather1(1, 4)
    back_product(2)
    gather3(0, 3)
    gather3(0, 4)
    scatter_x(1)
    back_product(0)
    gather2(1, 2)
    scatter_x(2)
    gather2(1, 0)
    gather2(1, 3)
    scatter_x(0)
    gather2(1, 4)
    back_product(4)
    back_product(3)
    scatter_x(4)
    scatter_z(1)
    gather2(1, 1)
    scatter_z(2)
    scatter_x(3)
    gather3(1, 0)
    gather3(1, 2)
    scatter_z(4)
    scatter_z(3)
    scatter_z(0)
    gather3(1, 3)
    gather3(1, 1)
    gather3(1, 4)
    grad_in()
    scaled = total_back()
    partial_out()
    last_out()
    finish_input(scaled)

    for a in (0, 1):
        departed(("z", a), gath.at[a, pl.ds(0, 7), 0])
        departed(("k", a), gath.at[a, pl.ds(0, 7), 0])
        departed(("o", a), w_in.at[pl.ds(0, 96)])
        departed(("p", a), part.at[a, :, pl.ds(0, 256)])
        departed(("b", a), part.at[a, :, pl.ds(0, 256)])
        departed(("af", a), sa.at[a, pl.ds(0, 128)])
        departed(("a3", a), rbx.at[a])
        departed(("b3", a), rbx.at[a])
        departed(("g1", a), sb.at[a])
        departed(("h2", a), hid.at[a, :, pl.ds(0, 256)])
        departed(("g2", a), sa.at[a, pl.ds(0, 128)])
        departed(("g3", a), hid.at[a, :, pl.ds(0, 256)])
    departed(("n",), gs)
    departed(("x",), xs)
    departed(("s",), zs.at[pl.ds(1, 7)])
    departed(("st",), st.at[pl.ds(1, 7)])
    departed(("ft",), ft.at[pl.ds(1, 7)])


def deliver(*refs):
    for source, target in zip(refs[:4], refs[4:]):
        target[...] = source[...]


def local(inputs, gain, w_in, bias, w_out, cotangent):
    vmem = pl.BlockSpec(memory_space=pltpu.VMEM)
    anywhere = pl.BlockSpec(memory_space=pl.ANY)
    shapes = (
        jax.ShapeDtypeStruct((32, BLK), BF16),
        jax.ShapeDtypeStruct((BLK, BLK), BF16),
        jax.ShapeDtypeStruct((BLK,), F32),
        jax.ShapeDtypeStruct((BLK, BLK), BF16),
    )
    results = pl.pallas_call(
        kernel,
        out_shape=shapes,
        in_specs=[anywhere] * 6,
        out_specs=[vmem] * 4,
        scratch_shapes=[
            pltpu.VMEM((32, BLK), BF16),
            pltpu.VMEM((1, BLK), F32),
            pltpu.VMEM((BLK, BLK), BF16),
            pltpu.VMEM((1, BLK), F32),
            pltpu.VMEM((BLK, BLK), BF16),
            pltpu.VMEM((2, 8, 2, 64, BLK), BF16),
            pltpu.VMEM((2, TOKENS, BLK), BF16),
            pltpu.VMEM((2, TOKENS // 2, CA), BF16),
            pltpu.VMEM((2, TOKENS // 2, CA), BF16),
            pltpu.VMEM((2, 2, TOKENS // 8, HA), BF16),
            pltpu.VMEM((2, 2, TOKENS // 8, CA), BF16),
            pltpu.VMEM((2, 2, TOKENS // 4, HB), BF16),
            pltpu.VMEM((2, 2, TOKENS // 4, CB), BF16),
            pltpu.VMEM((2, TOKENS // 4, CB), BF16),
            pltpu.VMEM((2, TOKENS // 8, CB), BF16),
            pltpu.VMEM((2, TOKENS, BLK), BF16),
            pltpu.VMEM((8, 64, BLK), F32),
            pltpu.VMEM((8, 64, BLK), BF16),
            pltpu.VMEM((8, 64, BLK), BF16),
            pltpu.VMEM((8, 32, BLK), BF16),
            pltpu.VMEM((8, 32, BLK), BF16),
            pltpu.VMEM((8, 32, BLK), BF16),
            pltpu.VMEM((8, 32, BLK), BF16),
            pltpu.VMEM((BLK, BLK), F32),
            pltpu.VMEM((8, 32, 128), F32),
            pltpu.VMEM((8, 32, 128), F32),
            pltpu.SemaphoreType.DMA((6,)),
            pltpu.SemaphoreType.DMA((N_SEND,)),
            pltpu.SemaphoreType.DMA((N_RECV,)),
        ],
        compiler_params=pltpu.CompilerParams(
            collective_id=0, has_side_effects=True, vmem_limit_bytes=56 * 2**20
        ),
        name="mlp_backward",
    )(inputs, gain, w_in, bias, w_out, cotangent)
    return pl.pallas_call(
        deliver,
        out_shape=shapes,
        in_specs=[vmem] * 4,
        out_specs=[vmem] * 4,
        name="deliver",
    )(*results)


def solution(mesh):
    in_specs = (
        P("col", "row"),
        P("row"),
        P("row", "col"),
        P("col"),
        P("col", "row"),
        P("col", "row"),
    )
    out_specs = (P("col", "row"), P("row", "col"), P("col"), P("col", "row"))
    return jax.shard_map(local, mesh=mesh, in_specs=in_specs, out_specs=out_specs, check_vma=False)
```

```python
import functools

import jax
import jax.numpy as jnp
from jax import lax
from jax.experimental import pallas as pl
from jax.experimental.pallas import tpu as pltpu
from jax.sharding import PartitionSpec as P

MESH = pl.DeviceIdType.MESH
F32, BF16 = jnp.float32, jnp.bfloat16
D = 6144
EPS = 1e-06
TOKENS, BLK = 1024, 768
CA = 256
CB = BLK - CA
HA, HB = CA // 2, CB // 2
COLS_A, COLS_B = pl.ds(0, CA), pl.ds(CA, CB)
DELTA = (0, 1, -1, 2, -2, 3, -3, 4)
CHUNKS = ((0, 1), (1, 3), (3, 5), (5, 7), (7, 8))
N_SEND, N_RECV = 40, 200


def normal_parts(pre_act):
    cumulative = 0.5 * (1.0 + lax.erf(pre_act * 0.7071067811865476))
    density = jnp.exp(-0.5 * pre_act * pre_act) * 0.3989422804014327
    return cumulative, density


def slot_of(delta):
    return DELTA.index(4 if delta in (4, -4) else delta)


def kernel(
    inp_hbm, gain_hbm, w_in_hbm, bias_hbm, w_out_hbm, cot_hbm, gi, gwi, gb, gwo,
    inp, gain, w_in, bias, w_out, gath, part, ra1, sa, raf, ra3, rbf, rb, sb, rbx, hid,
    gk, gs, gr, xs, xr, zs, zr, acc, st, ft, load_sem, send_sem, recv_sem,
):
    row, col = lax.axis_index("row"), lax.axis_index("col")
    y, xl = row // 2, row % 2
    xh, z, k = col // 16, (col // 2) % 8, col % 2

    def dev(dy=0, dx=0, dh=0, dz=0, dk=0):
        return (
            ((y + dy + 4) % 4) * 2 + (xl + dx) % 2,
            ((xh + dh) % 2) * 16 + ((z + dz + 8) % 8) * 2 + (k + dk) % 2,
        )

    xp, yp, ym, y2 = 1 - xl, (y + 1) % 4, (y + 3) % 4, (y + 2) % 4
    ROW_PEERS = [(dy, dx) for dy in range(4) for dx in range(2) if dy or dx]
    partners = [dev(dy=a, dx=b) for a, b in ROW_PEERS]
    partners += [dev(dz=1), dev(dz=-1), dev(dk=1), dev(dh=1), dev(dh=1, dk=1)]
    barrier = pltpu.get_barrier_semaphore()
    for partner in partners:
        pl.semaphore_signal(barrier, inc=1, device_id=partner, device_id_type=MESH)
    loads = [
        pltpu.make_async_copy(src, dst, load_sem.at[i])
        for i, (src, dst) in enumerate((
            (cot_hbm, gath.at[0, 0, 0, pl.ds(0, 32)]),
            (inp_hbm, inp),
            (gain_hbm, gain.at[0]),
            (bias_hbm, bias.at[0]),
            (w_out_hbm, w_out),
            (w_in_hbm, w_in),
        ))
    ]
    for load in loads:
        load.start()

    send_index, recv_index = {}, {}

    def send(key, kind, src, dst, to):
        pltpu.make_async_remote_copy(
            src_ref=src, dst_ref=dst,
            send_sem=send_sem.at[send_index.setdefault(kind, len(send_index))],
            recv_sem=recv_sem.at[recv_index.setdefault(key, len(recv_index))],
            device_id=to, device_id_type=MESH,
        ).start()

    def all_of(ref, kind, key):
        return pltpu.make_async_remote_copy(
            src_ref=ref, dst_ref=ref, send_sem=send_sem.at[send_index[kind]],
            recv_sem=recv_sem.at[recv_index[key]], device_id=dev(dk=1), device_id_type=MESH,
        )

    def arrived(key, ref):
        all_of(ref, ("st",), key).wait_recv()

    def departed(kind, ref):
        all_of(ref, kind, ("st",)).wait_send()

    lane = lax.broadcasted_iota(jnp.int32, (32, 128), 1)

    def pair(a, b):
        return jnp.where(lane < 64, a, b)

    loads[0].wait()
    loads[1].wait()
    values = inp[...].astype(F32)
    st[0] = pair(
        jnp.sum(values, 1, keepdims=True), jnp.sum(values * values, 1, keepdims=True)
    )
    pl.semaphore_wait(barrier, len(partners))

    def all_row(tag, ref):
        for i, (dy, dx) in enumerate(ROW_PEERS):
            send((tag,), (tag,), ref.at[0], ref.at[i + 1], dev(dy=dy, dx=dx))

    def row_sum(tag, ref):
        arrived((tag,), ref.at[pl.ds(1, 7)])
        total = ref[0]
        for i in range(1, 8):
            total = total + ref[i]
        return total[:, 0:1] * (1.0 / D), total[:, 64:65] * (1.0 / D)

    def unit(a, slot, u):
        return gath.at[a, slot, 0, pl.ds(u * 32, 32)]

    def pass_z(a, u, origin, slot, dz):
        send(("z", a, u, slot), ("z", a), unit(a, origin, u), unit(a, slot, u), dev(dz=dz))

    def z_first(a, u):
        pass_z(a, u, 0, 2, 1)
        pass_z(a, u, 0, 1, -1)

    def to_sibling(a, c, slot, u):
        mine = unit(a, slot, u)
        send(("k", a, c), ("k", a), mine, gath.at[a, slot, 1, pl.ds(u * 32, 32)], dev(dk=1))

    def own(a):
        mine = unit(a, 0, 0)
        send(("h", a), ("o", a), mine, unit(a, 0, 1), dev(dh=1))
        z_first(a, 0)
        send(("k", a, 0), ("o", a), mine, gath.at[a, 0, 1, pl.ds(32, 32)], dev(dh=1, dk=1))
        send(("k", a, 0), ("o", a), mine, gath.at[a, 0, 1, pl.ds(0, 32)], dev(dk=1))

    def other(a):
        arrived(("h", a), unit(a, 0, 1))
        z_first(a, 1)

    def hop(a, u, h):
        if h == 4:
            arrived(("z", a, u, 7), unit(a, 7, u))
            to_sibling(a, h, 7, u)
            return
        for slot, dz in ((slot_of(-h), 1), (slot_of(h), -1)):
            arrived(("z", a, u, slot), unit(a, slot, u))
            if h < 3 or u == (dz < 0):
                pass_z(a, u, slot, slot_of(-dz * (h + 1)), dz)
            to_sibling(a, h, slot, u)

    def span(c):
        s0, s1 = CHUNKS[c]
        return s0 * 128, (s1 - s0) * 128

    def at(base, index, size):
        return pl.ds(pl.multiple_of(base + index * size, 16), size)

    def product(a, c):
        off, t = span(c)
        s0, s1 = CHUNKS[c]
        arrived(("k", a, c), gath.at[a, pl.ds(s0, s1 - s0), 1])
        rows = gath[a, s0:s1].reshape(t, BLK)
        if a == 0:
            out = lax.dot_general(
                rows, w_out[...], (((1,), (1,)), ((), ())), preferred_element_type=F32
            )
        else:
            out = jnp.dot(rows, w_in[...], preferred_element_type=F32)
        part[a, off:off + t, :] = out.astype(BF16)
        far = at(off, y2, t // 4)
        quarter = pl.ds(off // 4, t // 4)
        for i, dy in ((0, 1), (1, -1)):
            send(
                ("bf", a, c), ("p", a), part.at[a, far, pl.ds(CA + i * HB, HB)],
                rbf.at[a, i, quarter], dev(dy=dy),
            )
        send(
            ("a1", a, c), ("p", a), part.at[a, at(off, xp, t // 2), COLS_A],
            ra1.at[a, pl.ds(off // 2, t // 2)], dev(dx=1),
        )

    def merge(ref, a, rows, cols, other):
        ref[a, rows, cols] = (ref[a, rows, cols].astype(F32) + other.astype(F32)).astype(BF16)

    def reduce2(a, c):
        off, t = span(c)
        o2, o4, o8, t2, t4, t8 = off // 2, off // 4, off // 8, t // 2, t // 4, t // 8
        arrived(("bf", a, c), rbf.at[a, :, pl.ds(o4, t4)])
        for i, block, start, dy in ((0, yp, CA, 1), (1, ym, CA + HB, -1)):
            merge(part, a, at(off, block, t4), pl.ds(start, HB), rbf[a, i, o4:o4 + t4])
            send(
                ("b", a, c), ("b", a), part.at[a, at(off, block, t4), COLS_B],
                rb.at[a, i, pl.ds(o4, t4)], dev(dy=dy),
            )
        arrived(("a1", a, c), ra1.at[a, pl.ds(o2, t2)])
        total = part[a, at(off, xl, t2), COLS_A].astype(F32) + ra1[a, o2:o2 + t2].astype(F32)
        sa[a, o2:o2 + t2] = total.astype(BF16)
        for i, dy in ((0, 1), (1, -1)):
            send(
                ("af", a, c), ("af", a), sa.at[a, at(o2, y2, t8), pl.ds(i * HA, HA)],
                raf.at[a, i, pl.ds(o8, t8)], dev(dy=dy),
            )

    def reduce3(a, c):
        off, t = span(c)
        o2, o4, o8, t4, t8 = off // 2, off // 4, off // 8, t // 4, t // 8
        arrived(("af", a, c), raf.at[a, :, pl.ds(o8, t8)])
        for i, block, start, dy in ((0, yp, 0, 1), (1, ym, HA, -1)):
            merge(sa, a, at(o2, block, t8), pl.ds(start, HA), raf[a, i, o8:o8 + t8])
            send(
                ("a3", a, c), ("a3", a), sa.at[a, at(o2, block, t8)],
                ra3.at[a, i, pl.ds(o8, t8)], dev(dy=dy),
            )
        arrived(("b", a, c), rb.at[a, :, pl.ds(o4, t4)])
        total = part[a, at(off, y, t4), COLS_B].astype(F32)
        for i in (0, 1):
            total = total + rb[a, i, o4:o4 + t4].astype(F32)
        sb[a, o4:o4 + t4] = total.astype(BF16)
        send(
            ("b3", a, c), ("b3", a), sb.at[a, at(o4, xp, t8)], rbx.at[a, pl.ds(o8, t8)],
            dev(dx=1),
        )

    def rows_a(c):
        off, t = span(c)
        return at(off, xl * 4 + y, t // 8)

    def rows_b(c):
        off, t = span(c)
        return at(off, y * 2 + xl, t // 8)

    def elementwise(c):
        off, t = span(c)
        o2, o4, o8, t8 = off // 2, off // 4, off // 8, t // 8

        def finish(rows, cols, bias_part, totals):
            pre_act = totals[1] + bias_part
            cumulative, density = normal_parts(pre_act)
            hid[0, rows, cols] = (totals[0] * (cumulative + pre_act * density)).astype(BF16)
            hid[1, rows, cols] = (pre_act * cumulative).astype(BF16)

        totals = []
        for a in (0, 1):
            arrived(("a3", a, c), ra3.at[a, :, pl.ds(o8, t8)])
            total = sa[a, at(o2, y, t8)].astype(F32)
            for i in (0, 1):
                total = total + ra3[a, i, o8:o8 + t8].astype(F32)
            totals.append(total)
        finish(rows_a(c), COLS_A, bias[:, 0:CA], totals)
        totals = []
        for a in (0, 1):
            arrived(("b3", a, c), rbx.at[a, pl.ds(o8, t8)])
            totals.append(sb[a, at(o4, xl, t8)].astype(F32) + rbx[a, o8:o8 + t8].astype(F32))
        finish(rows_b(c), COLS_B, bias[:, CA:BLK], totals)

    def share(key, kind, ref, to):
        send(key, kind, ref, ref, to)

    def block_a(g, c, index, cols=COLS_A):
        off, t = span(c)
        return hid.at[g, at(off, xl * 4 + index, t // 8), cols]

    def block_b(g, c, index, cols=COLS_B):
        off, t = span(c)
        return hid.at[g, at(off, index, t // 4), cols]

    def gather1(g, c):
        share(("h1", g, c), ("g1", g), hid.at[g, rows_b(c), COLS_B], dev(dx=1))
        for i, dy in ((0, 1), (1, -1)):
            share(("g1", g, c, i), ("g1", g), block_a(g, c, y), dev(dy=dy))

    def gather2(g, c):
        off, t = span(c)
        arrived(("h1", g, c), hid.at[g, at(off, y * 2 + xp, t // 8), COLS_B])
        for i, dy in ((0, 1), (1, -1)):
            share(("h2", g, c, i), ("h2", g), block_b(g, c, y), dev(dy=dy))
        for i, block, dy in ((0, ym, 1), (1, yp, -1)):
            arrived(("g1", g, c, i), block_a(g, c, block))
            share(("g2", g, c), ("g2", g), block_a(g, c, block, pl.ds(i * HA, HA)), dev(dy=dy))

    def gather3(g, c):
        off, t = span(c)
        for i, block, dy in ((0, ym, 1), (1, yp, -1)):
            arrived(("h2", g, c, i), block_b(g, c, block))
            share(("h3", g, c), ("g3", g), block_b(g, c, block, pl.ds(CA + i * HB, HB)), dev(dy=dy))
        arrived(("g2", g, c), block_a(g, c, y2))
        share(("g3", g, c), ("g3", g), hid.at[g, at(off, xl, t // 2), COLS_A], dev(dx=1))

    def gathered(g, c):
        off, t = span(c)
        arrived(("g3", g, c), hid.at[g, at(off, xp, t // 2), COLS_A])
        arrived(("h3", g, c), block_b(g, c, y2))

    ready = set()

    def all_gathered(g, chunks):
        for c in chunks:
            if (g, c) not in ready:
                ready.add((g, c))
                gathered(g, c)

    def back_product(c):
        all_gathered(0, (c,))
        off, t = span(c)
        s0, s1 = CHUNKS[c]
        out = lax.dot_general(
            hid[0, off:off + t, :], w_in[...], (((1,), (1,)), ((), ())),
            preferred_element_type=F32,
        )
        for slot in range(s0, s1):
            base = (slot - s0) * 128
            gk[slot] = out[base:base + 64]
            gs[slot] = out[base + 64:base + 128].astype(BF16)
        send(("n", c), ("n",), gs.at[pl.ds(s0, s1 - s0)], gr.at[pl.ds(s0, s1 - s0)], dev(dk=1))

    def scatter_x(c):
        s0, s1 = CHUNKS[c]
        arrived(("n", c), gr.at[pl.ds(s0, s1 - s0)])
        for slot in range(s0, s1):
            total = gk[slot] + gr[slot].astype(F32)
            gk[slot, 0:32] = total[0:32]
            xs[slot] = total[32:64].astype(BF16)
        send(("x", c), ("x",), xs.at[pl.ds(s0, s1 - s0)], xr.at[pl.ds(s0, s1 - s0)], dev(dh=1))

    def scatter_z(c):
        s0, s1 = CHUNKS[c]
        arrived(("x", c), xr.at[pl.ds(s0, s1 - s0)])
        for slot in range(s0, s1):
            total = gk[slot, 0:32] + xr[slot].astype(F32)
            if slot == 0:
                gk[0, 0:32] = total
            else:
                zs[slot] = total.astype(BF16)
                send(("s",), ("s",), zs.at[slot], zr.at[slot], dev(dz=DELTA[slot]))

    scale = float(TOKENS) ** (-0.5)
    tiles = [(i * 256, (i + 1) * 256) for i in range(3)]

    def outer(left, right):
        return lax.dot_general(
            left, right, (((0,), (0,)), ((), ())), preferred_element_type=F32
        )

    def flat(a, s0=0, s1=8):
        return gath[a, s0:s1].reshape((s1 - s0) * 128, BLK)

    def grad_in(n):
        all_gathered(0, range(5))
        i, j = tiles[n]
        gwi[i:j, :] = (outer(flat(1)[:, i:j], hid[0]) * scale).astype(BF16)
        if n == 0:
            gb[...] = (jnp.sum(hid[0].astype(F32), 0, keepdims=True) * scale).reshape(BLK)

    def total_back():
        total = gk[0, 0:32]
        arrived(("s",), zr.at[pl.ds(1, 7)])
        for slot in range(1, 8):
            total = total + zr[slot].astype(F32)
        scaled = total * gain[...]
        ft[0] = pair(
            jnp.sum(scaled, 1, keepdims=True), jnp.sum(scaled * centred, 1, keepdims=True)
        )
        all_row("ft", ft)
        return scaled

    def finish_input(scaled):
        first, cross = row_sum("ft", ft)
        gi[...] = (inv_std * (scaled - first - centred * cross)).astype(BF16)

    def partial_out(n):
        all_gathered(1, (2 * n, 2 * n + 1))
        s0, s1 = CHUNKS[2 * n][0], CHUNKS[2 * n + 1][1]
        for i, j in tiles:
            part_sum = outer(hid[1, s0 * 128:s1 * 128, i:j], flat(0, s0, s1))
            acc[i:j, :] = acc[i:j, :] + part_sum if n else part_sum

    def last_out():
        all_gathered(1, (4,))
        for i, j in tiles:
            gwo[i:j, :] = (
                (acc[i:j, :] + outer(hid[1, 896:TOKENS, i:j], flat(0, 7, 8))) * scale
            ).astype(BF16)

    own(0)
    all_row("st", st)
    mean_x, second = row_sum("st", st)
    inv_std = lax.rsqrt(second - mean_x * mean_x + EPS)
    centred = (values - mean_x) * inv_std
    loads[2].wait()
    gath[1, 0, 0, 0:32] = (centred * gain[...]).astype(BF16)
    own(1)
    other(0)
    hop(0, 0, 1)
    loads[4].wait()
    product(0, 0)
    other(1)
    loads[5].wait()
    product(1, 0)
    hop(0, 1, 1)
    hop(1, 0, 1)
    reduce2(0, 0)
    product(0, 1)
    hop(1, 1, 1)
    hop(0, 0, 2)
    reduce2(1, 0)
    hop(0, 1, 2)
    product(1, 1)
    reduce3(0, 0)
    product(0, 2)
    hop(1, 0, 2)
    reduce2(0, 1)
    hop(1, 1, 2)
    reduce3(1, 0)
    hop(0, 0, 3)
    product(1, 2)
    reduce2(1, 1)
    hop(0, 1, 3)
    reduce2(0, 2)
    hop(1, 1, 3)
    hop(1, 0, 3)
    product(0, 3)
    product(1, 3)
    reduce2(1, 2)
    loads[3].wait()
    elementwise(0)
    reduce3(1, 1)
    hop(1, 0, 4)
    hop(0, 0, 4)
    reduce3(0, 1)
    hop(0, 1, 4)
    reduce2(0, 3)
    product(0, 4)
    hop(1, 1, 4)
    product(1, 4)
    reduce2(1, 3)
    elementwise(1)
    reduce3(0, 2)
    reduce3(1, 2)
    gather1(0, 1)
    reduce2(1, 4)
    reduce3(0, 3)
    reduce2(0, 4)
    reduce3(1, 3)
    elementwise(2)
    gather1(0, 2)
    gather2(0, 1)
    gather1(0, 0)
    gather1(1, 0)
    reduce3(1, 4)
    reduce3(0, 4)
    elementwise(3)
    gather1(0, 3)
    gather2(0, 2)
    gather1(1, 1)
    gather3(0, 1)
    elementwise(4)
    gather1(0, 4)
    gather2(0, 3)
    gather3(0, 2)
    gather2(0, 4)
    back_product(1)
    gather1(1, 3)
    gather3(0, 3)
    back_product(2)
    gather3(0, 4)
    scatter_x(1)
    gather2(1, 0)
    gather2(0, 0)
    scatter_x(2)
    gather1(1, 4)
    gather2(1, 1)
    back_product(4)
    gather2(1, 3)
    gather1(1, 2)
    back_product(3)
    scatter_x(4)
    scatter_z(1)
    gather3(0, 0)
    gather2(1, 4)
    scatter_z(2)
    scatter_x(3)
    gather3(1, 0)
    scatter_z(4)
    gather2(1, 2)
    back_product(0)
    gather3(1, 1)
    grad_in(1)
    scatter_x(0)
    scatter_z(3)
    gather3(1, 3)
    grad_in(2)
    gather3(1, 2)
    gather3(1, 4)
    partial_out(0)
    grad_in(0)
    scatter_z(0)
    scaled = total_back()
    partial_out(1)
    last_out()
    finish_input(scaled)

    for a in (0, 1):
        departed(("z", a), gath.at[a, pl.ds(0, 7), 0])
        departed(("k", a), gath.at[a, pl.ds(0, 7), 0])
        departed(("o", a), w_in.at[pl.ds(0, 96)])
        departed(("p", a), part.at[a, :, pl.ds(0, 256)])
        departed(("b", a), part.at[a, :, pl.ds(0, 256)])
        departed(("af", a), sa.at[a, pl.ds(0, 128)])
        departed(("a3", a), rbx.at[a])
        departed(("b3", a), rbx.at[a])
        departed(("g1", a), sb.at[a])
        departed(("h2", a), hid.at[a, :, pl.ds(0, 256)])
        departed(("g2", a), sa.at[a, pl.ds(0, 128)])
        departed(("g3", a), hid.at[a, :, pl.ds(0, 256)])
    departed(("n",), gs)
    departed(("x",), xs)
    departed(("s",), zs.at[pl.ds(1, 7)])
    departed(("st",), st.at[pl.ds(1, 7)])
    departed(("ft",), ft.at[pl.ds(1, 7)])


def deliver(*refs):
    sources, targets, sem = refs[:4], refs[4:8], refs[8]
    copies = [
        pltpu.make_async_copy(src, dst, sem.at[i])
        for i, (src, dst) in enumerate(zip(sources, targets))
    ]
    for copy in copies:
        copy.start()
    for copy in copies:
        copy.wait()


def local(inputs, gain, w_in, bias, w_out, cotangent):
    vmem = pl.BlockSpec(memory_space=pltpu.VMEM)
    anywhere = pl.BlockSpec(memory_space=pl.ANY)
    shapes = (
        jax.ShapeDtypeStruct((32, BLK), BF16),
        jax.ShapeDtypeStruct((BLK, BLK), BF16),
        jax.ShapeDtypeStruct((BLK,), F32),
        jax.ShapeDtypeStruct((BLK, BLK), BF16),
    )
    results = pl.pallas_call(
        kernel,
        out_shape=tuple(pltpu.VMEM(x.shape, x.dtype) for x in shapes),
        in_specs=[anywhere] * 6,
        out_specs=[vmem] * 4,
        scratch_shapes=[
            pltpu.VMEM((32, BLK), BF16),
            pltpu.VMEM((1, BLK), F32),
            pltpu.VMEM((BLK, BLK), BF16),
            pltpu.VMEM((1, BLK), F32),
            pltpu.VMEM((BLK, BLK), BF16),
            pltpu.VMEM((2, 8, 2, 64, BLK), BF16),
            pltpu.VMEM((2, TOKENS, BLK), BF16),
            pltpu.VMEM((2, TOKENS // 2, CA), BF16),
            pltpu.VMEM((2, TOKENS // 2, CA), BF16),
            pltpu.VMEM((2, 2, TOKENS // 8, HA), BF16),
            pltpu.VMEM((2, 2, TOKENS // 8, CA), BF16),
            pltpu.VMEM((2, 2, TOKENS // 4, HB), BF16),
            pltpu.VMEM((2, 2, TOKENS // 4, CB), BF16),
            pltpu.VMEM((2, TOKENS // 4, CB), BF16),
            pltpu.VMEM((2, TOKENS // 8, CB), BF16),
            pltpu.VMEM((2, TOKENS, BLK), BF16),
            pltpu.VMEM((8, 64, BLK), F32),
            pltpu.VMEM((8, 64, BLK), BF16),
            pltpu.VMEM((8, 64, BLK), BF16),
            pltpu.VMEM((8, 32, BLK), BF16),
            pltpu.VMEM((8, 32, BLK), BF16),
            pltpu.VMEM((8, 32, BLK), BF16),
            pltpu.VMEM((8, 32, BLK), BF16),
            pltpu.VMEM((BLK, BLK), F32),
            pltpu.VMEM((8, 32, 128), F32),
            pltpu.VMEM((8, 32, 128), F32),
            pltpu.SemaphoreType.DMA((6,)),
            pltpu.SemaphoreType.DMA((N_SEND,)),
            pltpu.SemaphoreType.DMA((N_RECV,)),
        ],
        compiler_params=pltpu.CompilerParams(
            collective_id=0, has_side_effects=True, vmem_limit_bytes=56 * 2**20
        ),
        name="mlp_backward",
    )(inputs, gain, w_in, bias, w_out, cotangent)
    return pl.pallas_call(
        deliver,
        out_shape=shapes,
        in_specs=[vmem] * 4,
        out_specs=[anywhere] * 4,
        scratch_shapes=[pltpu.SemaphoreType.DMA((4,))],
        compiler_params=pltpu.CompilerParams(vmem_limit_bytes=4 * 2**20),
        name="deliver",
    )(*results)


def solution(mesh):
    in_specs = (
        P("col", "row"),
        P("row"),
        P("row", "col"),
        P("col"),
        P("col", "row"),
        P("col", "row"),
    )
    out_specs = (P("col", "row"), P("row", "col"), P("col"), P("col", "row"))
    return jax.shard_map(local, mesh=mesh, in_specs=in_specs, out_specs=out_specs, check_vma=False)
```

```python
import functools

import jax
import jax.numpy as jnp
from jax import lax
from jax.experimental import pallas as pl
from jax.experimental.pallas import tpu as pltpu
from jax.sharding import PartitionSpec as P

MESH = pl.DeviceIdType.MESH
F32, BF16 = jnp.float32, jnp.bfloat16
D = 6144
EPS = 1e-06
TOKENS, BLK = 1024, 768
CA = 256
CB = BLK - CA
HA, HB = CA // 2, CB // 2
COLS_A, COLS_B = pl.ds(0, CA), pl.ds(CA, CB)
DELTA = (0, 1, -1, 2, -2, 3, -3, 4)
CHUNKS = ((0, 1), (1, 3), (3, 5), (5, 7), (7, 8))
LAST = len(CHUNKS) - 1
N_SEND, N_RECV = 40, 200


def normal_parts(pre_act):
    cumulative = 0.5 * (1.0 + lax.erf(pre_act * 0.7071067811865476))
    density = jnp.exp(-0.5 * pre_act * pre_act) * 0.3989422804014327
    return cumulative, density


def slot_of(delta):
    return DELTA.index(4 if delta in (4, -4) else delta)


def kernel(
    inp_hbm, gain_hbm, w_in_hbm, bias_hbm, w_out_hbm, cot_hbm, gi, gwi, gb, gwo,
    inp, gain, w_in, bias, w_out, gath, part, ra1, sa, raf, ra3, rbf, rb, sb, rbx, hid,
    gk, gs, gr, xs, xr, zs, zr, acc, st, ft, load_sem, send_sem, recv_sem,
):
    row, col = lax.axis_index("row"), lax.axis_index("col")
    y, xl = row // 2, row % 2
    xh, z, k = col // 16, (col // 2) % 8, col % 2

    def dev(dy=0, dx=0, dh=0, dz=0, dk=0):
        return (
            ((y + dy + 4) % 4) * 2 + (xl + dx) % 2,
            ((xh + dh) % 2) * 16 + ((z + dz + 8) % 8) * 2 + (k + dk) % 2,
        )

    xp, yp, ym, y2 = 1 - xl, (y + 1) % 4, (y + 3) % 4, (y + 2) % 4
    ROW_PEERS = [(dy, dx) for dy in range(4) for dx in range(2) if dy or dx]
    partners = [dev(dy=a, dx=b) for a, b in ROW_PEERS]
    partners += [dev(dz=1), dev(dz=-1), dev(dk=1), dev(dh=1), dev(dh=1, dk=1)]
    barrier = pltpu.get_barrier_semaphore()
    for partner in partners:
        pl.semaphore_signal(barrier, inc=1, device_id=partner, device_id_type=MESH)
    loads = [
        pltpu.make_async_copy(src, dst, load_sem.at[i])
        for i, (src, dst) in enumerate((
            (cot_hbm, gath.at[0, 0, 0, pl.ds(0, 32)]),
            (inp_hbm, inp),
            (gain_hbm, gain.at[0]),
            (bias_hbm, bias.at[0]),
            (w_out_hbm, w_out),
            (w_in_hbm, w_in),
        ))
    ]
    for load in loads:
        load.start()

    send_index, recv_index = {}, {}

    def send(key, kind, src, dst, to):
        pltpu.make_async_remote_copy(
            src_ref=src, dst_ref=dst,
            send_sem=send_sem.at[send_index.setdefault(kind, len(send_index))],
            recv_sem=recv_sem.at[recv_index.setdefault(key, len(recv_index))],
            device_id=to, device_id_type=MESH,
        ).start()

    def all_of(ref, kind, key):
        return pltpu.make_async_remote_copy(
            src_ref=ref, dst_ref=ref, send_sem=send_sem.at[send_index[kind]],
            recv_sem=recv_sem.at[recv_index[key]], device_id=dev(dk=1), device_id_type=MESH,
        )

    def arrived(key, ref):
        all_of(ref, ("st",), key).wait_recv()

    def departed(kind, ref):
        all_of(ref, kind, ("st",)).wait_send()

    lane = lax.broadcasted_iota(jnp.int32, (32, 128), 1)

    def pair(a, b):
        columns = jnp.where(lane < 64, a, b)
        return jnp.concatenate([columns, jnp.zeros((96, 128), F32)], 0).T[60:68]

    loads[0].wait()
    loads[1].wait()
    values = inp[...].astype(F32)
    st[0] = pair(
        jnp.sum(values, 1, keepdims=True), jnp.sum(values * values, 1, keepdims=True)
    )
    pl.semaphore_wait(barrier, len(partners))

    def all_row(tag, ref):
        for i, (dy, dx) in enumerate(ROW_PEERS):
            send((tag,), (tag,), ref.at[0], ref.at[i + 1], dev(dy=dy, dx=dx))

    def row_sum(tag, ref):
        arrived((tag,), ref.at[pl.ds(1, 7)])
        total = ref[0]
        for i in range(1, 8):
            total = total + ref[i]
        columns = jnp.concatenate([total, jnp.zeros((120, 128), F32)], 0).T
        return columns[0:32, 0:1] * (1.0 / D), columns[0:32, 4:5] * (1.0 / D)

    def unit(a, slot, u):
        return gath.at[a, slot, 0, pl.ds(u * 32, 32)]

    def pass_z(a, u, origin, slot, dz):
        send(("z", a, u, slot), ("z", a), unit(a, origin, u), unit(a, slot, u), dev(dz=dz))

    def z_first(a, u):
        pass_z(a, u, 0, 2, 1)
        pass_z(a, u, 0, 1, -1)

    def to_sibling(a, h, slot, u):
        mine = unit(a, slot, u)
        send(("k", a, min(h, LAST)), ("k", a), mine, gath.at[a, slot, 1, pl.ds(u * 32, 32)], dev(dk=1))

    def own(a):
        mine = unit(a, 0, 0)
        send(("h", a), ("o", a), mine, unit(a, 0, 1), dev(dh=1))
        z_first(a, 0)
        send(("k", a, 0), ("o", a), mine, gath.at[a, 0, 1, pl.ds(32, 32)], dev(dh=1, dk=1))
        send(("k", a, 0), ("o", a), mine, gath.at[a, 0, 1, pl.ds(0, 32)], dev(dk=1))

    def other(a):
        arrived(("h", a), unit(a, 0, 1))
        z_first(a, 1)

    def hop(a, u, h):
        if h == 4:
            arrived(("z", a, u, 7), unit(a, 7, u))
            to_sibling(a, h, 7, u)
            return
        for slot, dz in ((slot_of(-h), 1), (slot_of(h), -1)):
            arrived(("z", a, u, slot), unit(a, slot, u))
            if h < 3 or u == (dz < 0):
                pass_z(a, u, slot, slot_of(-dz * (h + 1)), dz)
            to_sibling(a, h, slot, u)

    def span(c):
        s0, s1 = CHUNKS[c]
        return s0 * 128, (s1 - s0) * 128

    def at(base, index, size):
        return pl.ds(pl.multiple_of(base + index * size, 16), size)

    def product(a, c):
        off, t = span(c)
        s0, s1 = CHUNKS[c]
        arrived(("k", a, c), gath.at[a, pl.ds(s0, s1 - s0), 1])
        rows = gath[a, s0:s1].reshape(t, BLK)
        if a == 0:
            out = lax.dot_general(
                rows, w_out[...], (((1,), (1,)), ((), ())), preferred_element_type=F32
            )
        else:
            out = jnp.dot(rows, w_in[...], preferred_element_type=F32)
        part[a, off:off + t, :] = out.astype(BF16)
        far = at(off, y2, t // 4)
        quarter = pl.ds(off // 4, t // 4)
        for i, dy in ((0, 1), (1, -1)):
            send(
                ("bf", a, c), ("p", a), part.at[a, far, pl.ds(CA + i * HB, HB)],
                rbf.at[a, i, quarter], dev(dy=dy),
            )
        send(
            ("a1", a, c), ("p", a), part.at[a, at(off, xp, t // 2), COLS_A],
            ra1.at[a, pl.ds(off // 2, t // 2)], dev(dx=1),
        )

    def merge(ref, a, rows, cols, other):
        ref[a, rows, cols] = (ref[a, rows, cols].astype(F32) + other.astype(F32)).astype(BF16)

    def reduce2(a, c):
        off, t = span(c)
        o2, o4, o8, t2, t4, t8 = off // 2, off // 4, off // 8, t // 2, t // 4, t // 8
        arrived(("bf", a, c), rbf.at[a, :, pl.ds(o4, t4)])
        for i, block, start, dy in ((0, yp, CA, 1), (1, ym, CA + HB, -1)):
            merge(part, a, at(off, block, t4), pl.ds(start, HB), rbf[a, i, o4:o4 + t4])
            send(
                ("b", a, c), ("b", a), part.at[a, at(off, block, t4), COLS_B],
                rb.at[a, i, pl.ds(o4, t4)], dev(dy=dy),
            )
        arrived(("a1", a, c), ra1.at[a, pl.ds(o2, t2)])
        total = part[a, at(off, xl, t2), COLS_A].astype(F32) + ra1[a, o2:o2 + t2].astype(F32)
        sa[a, o2:o2 + t2] = total.astype(BF16)
        for i, dy in ((0, 1), (1, -1)):
            send(
                ("af", a, c), ("af", a), sa.at[a, at(o2, y2, t8), pl.ds(i * HA, HA)],
                raf.at[a, i, pl.ds(o8, t8)], dev(dy=dy),
            )

    def reduce3(a, c):
        off, t = span(c)
        o2, o4, o8, t4, t8 = off // 2, off // 4, off // 8, t // 4, t // 8
        arrived(("af", a, c), raf.at[a, :, pl.ds(o8, t8)])
        for i, block, start, dy in ((0, yp, 0, 1), (1, ym, HA, -1)):
            merge(sa, a, at(o2, block, t8), pl.ds(start, HA), raf[a, i, o8:o8 + t8])
            send(
                ("a3", a, c), ("a3", a), sa.at[a, at(o2, block, t8)],
                ra3.at[a, i, pl.ds(o8, t8)], dev(dy=dy),
            )
        arrived(("b", a, c), rb.at[a, :, pl.ds(o4, t4)])
        total = part[a, at(off, y, t4), COLS_B].astype(F32)
        for i in (0, 1):
            total = total + rb[a, i, o4:o4 + t4].astype(F32)
        sb[a, o4:o4 + t4] = total.astype(BF16)
        send(
            ("b3", a, c), ("b3", a), sb.at[a, at(o4, xp, t8)], rbx.at[a, pl.ds(o8, t8)],
            dev(dx=1),
        )

    def rows_a(c):
        off, t = span(c)
        return at(off, xl * 4 + y, t // 8)

    def rows_b(c):
        off, t = span(c)
        return at(off, y * 2 + xl, t // 8)

    def elementwise(c):
        off, t = span(c)
        o2, o4, o8, t8 = off // 2, off // 4, off // 8, t // 8

        def finish(rows, cols, bias_part, totals):
            pre_act = totals[1] + bias_part
            cumulative, density = normal_parts(pre_act)
            hid[0, rows, cols] = (totals[0] * (cumulative + pre_act * density)).astype(BF16)
            hid[1, rows, cols] = (pre_act * cumulative).astype(BF16)

        totals = []
        for a in (0, 1):
            arrived(("a3", a, c), ra3.at[a, :, pl.ds(o8, t8)])
            total = sa[a, at(o2, y, t8)].astype(F32)
            for i in (0, 1):
                total = total + ra3[a, i, o8:o8 + t8].astype(F32)
            totals.append(total)
        finish(rows_a(c), COLS_A, bias[:, 0:CA], totals)
        totals = []
        for a in (0, 1):
            arrived(("b3", a, c), rbx.at[a, pl.ds(o8, t8)])
            totals.append(sb[a, at(o4, xl, t8)].astype(F32) + rbx[a, o8:o8 + t8].astype(F32))
        finish(rows_b(c), COLS_B, bias[:, CA:BLK], totals)

    def share(key, kind, ref, to):
        send(key, kind, ref, ref, to)

    def block_a(g, c, index, cols=COLS_A):
        off, t = span(c)
        return hid.at[g, at(off, xl * 4 + index, t // 8), cols]

    def block_b(g, c, index, cols=COLS_B):
        off, t = span(c)
        return hid.at[g, at(off, index, t // 4), cols]

    def gather1(g, c):
        share(("h1", g, c), ("g1", g), hid.at[g, rows_b(c), COLS_B], dev(dx=1))
        for i, dy in ((0, 1), (1, -1)):
            share(("g1", g, c, i), ("g1", g), block_a(g, c, y), dev(dy=dy))

    def gather2(g, c):
        off, t = span(c)
        arrived(("h1", g, c), hid.at[g, at(off, y * 2 + xp, t // 8), COLS_B])
        for i, dy in ((0, 1), (1, -1)):
            share(("h2", g, c, i), ("h2", g), block_b(g, c, y), dev(dy=dy))
        for i, block, dy in ((0, ym, 1), (1, yp, -1)):
            arrived(("g1", g, c, i), block_a(g, c, block))
            share(("g2", g, c), ("g2", g), block_a(g, c, block, pl.ds(i * HA, HA)), dev(dy=dy))

    def gather3(g, c):
        off, t = span(c)
        for i, block, dy in ((0, ym, 1), (1, yp, -1)):
            arrived(("h2", g, c, i), block_b(g, c, block))
            share(("h3", g, c), ("g3", g), block_b(g, c, block, pl.ds(CA + i * HB, HB)), dev(dy=dy))
        arrived(("g2", g, c), block_a(g, c, y2))
        share(("g3", g, c), ("g3", g), hid.at[g, at(off, xl, t // 2), COLS_A], dev(dx=1))

    def gathered(g, c):
        off, t = span(c)
        arrived(("g3", g, c), hid.at[g, at(off, xp, t // 2), COLS_A])
        arrived(("h3", g, c), block_b(g, c, y2))

    ready = set()

    def all_gathered(g, chunks):
        for c in chunks:
            if (g, c) not in ready:
                ready.add((g, c))
                gathered(g, c)

    def back_product(c):
        all_gathered(0, (c,))
        off, t = span(c)
        s0, s1 = CHUNKS[c]
        out = lax.dot_general(
            hid[0, off:off + t, :], w_in[...], (((1,), (1,)), ((), ())),
            preferred_element_type=F32,
        )
        for slot in range(s0, s1):
            base = (slot - s0) * 128
            gk[slot] = out[base:base + 64]
            gs[slot] = out[base + 64:base + 128].astype(BF16)
        send(("n", c), ("n",), gs.at[pl.ds(s0, s1 - s0)], gr.at[pl.ds(s0, s1 - s0)], dev(dk=1))

    def scatter_x(c):
        s0, s1 = CHUNKS[c]
        arrived(("n", c), gr.at[pl.ds(s0, s1 - s0)])
        for slot in range(s0, s1):
            total = gk[slot] + gr[slot].astype(F32)
            gk[slot, 0:32] = total[0:32]
            xs[slot] = total[32:64].astype(BF16)
        send(("x", c), ("x",), xs.at[pl.ds(s0, s1 - s0)], xr.at[pl.ds(s0, s1 - s0)], dev(dh=1))

    def scatter_z(c):
        s0, s1 = CHUNKS[c]
        arrived(("x", c), xr.at[pl.ds(s0, s1 - s0)])
        for slot in range(s0, s1):
            total = gk[slot, 0:32] + xr[slot].astype(F32)
            if slot == 0:
                gk[0, 0:32] = total
            else:
                zs[slot] = total.astype(BF16)
                send(("s",), ("s",), zs.at[slot], zr.at[slot], dev(dz=DELTA[slot]))

    scale = float(TOKENS) ** (-0.5)
    tiles = [(i * 256, (i + 1) * 256) for i in range(3)]

    def outer(left, right):
        return lax.dot_general(
            left, right, (((0,), (0,)), ((), ())), preferred_element_type=F32
        )

    def flat(a, s0=0, s1=8):
        return gath[a, s0:s1].reshape((s1 - s0) * 128, BLK)

    def grad_in(n):
        all_gathered(0, range(LAST + 1))
        i, j = tiles[n]
        gwi[i:j, :] = (outer(flat(1)[:, i:j], hid[0]) * scale).astype(BF16)
        if n == 0:
            gb[...] = (jnp.sum(hid[0].astype(F32), 0, keepdims=True) * scale).reshape(BLK)

    def total_back():
        total = gk[0, 0:32]
        arrived(("s",), zr.at[pl.ds(1, 7)])
        for slot in range(1, 8):
            total = total + zr[slot].astype(F32)
        scaled = total * gain[...]
        ft[0] = pair(
            jnp.sum(scaled, 1, keepdims=True), jnp.sum(scaled * centred, 1, keepdims=True)
        )
        all_row("ft", ft)
        return scaled

    def finish_input(scaled):
        first, cross = row_sum("ft", ft)
        gi[...] = (inv_std * (scaled - first - centred * cross)).astype(BF16)

    def rows_out(c, i, j):
        s0, s1 = CHUNKS[c]
        return outer(hid[1, s0 * 128:s1 * 128, i:j], flat(0, s0, s1))

    def partial_out(c):
        all_gathered(1, (c,))
        for i, j in tiles:
            acc[i:j, :] = acc[i:j, :] + rows_out(c, i, j) if c else rows_out(c, i, j)

    def last_out():
        all_gathered(1, (LAST,))
        for i, j in tiles:
            gwo[i:j, :] = ((acc[i:j, :] + rows_out(LAST, i, j)) * scale).astype(BF16)

    own(0)
    all_row("st", st)
    mean_x, second = row_sum("st", st)
    inv_std = lax.rsqrt(second - mean_x * mean_x + EPS)
    centred = (values - mean_x) * inv_std
    loads[2].wait()
    gath[1, 0, 0, 0:32] = (centred * gain[...]).astype(BF16)
    own(1)
    other(0)
    loads[4].wait()
    product(0, 0)
    hop(0, 0, 1)
    other(1)
    loads[5].wait()
    product(1, 0)
    hop(0, 1, 1)
    hop(1, 0, 1)
    reduce2(0, 0)
    product(0, 1)
    hop(1, 1, 1)
    hop(0, 0, 2)
    reduce2(1, 0)
    hop(0, 1, 2)
    product(1, 1)
    reduce3(0, 0)
    product(0, 2)
    reduce2(0, 1)
    hop(1, 0, 2)
    hop(1, 1, 2)
    reduce3(1, 0)
    product(1, 2)
    reduce2(1, 1)
    hop(0, 0, 3)
    hop(0, 1, 3)
    hop(1, 0, 3)
    reduce2(0, 2)
    product(0, 3)
    hop(1, 1, 3)
    reduce2(1, 2)
    loads[3].wait()
    elementwise(0)
    product(1, 3)
    hop(0, 0, 4)
    hop(1, 0, 4)
    reduce3(0, 2)
    reduce3(0, 1)
    reduce3(1, 1)
    reduce2(0, 3)
    hop(1, 1, 4)
    hop(0, 1, 4)
    product(1, 4)
    product(0, 4)
    reduce3(1, 2)
    reduce2(1, 3)
    gather1(0, 0)
    elementwise(1)
    gather1(0, 1)
    reduce3(0, 3)
    reduce2(0, 4)
    reduce2(1, 4)
    elementwise(2)
    gather1(0, 2)
    reduce3(1, 3)
    gather2(0, 1)
    gather2(0, 0)
    reduce3(0, 4)
    gather1(1, 0)
    reduce3(1, 4)
    elementwise(3)
    gather1(0, 3)
    gather2(0, 2)
    gather3(0, 1)
    elementwise(4)
    gather1(0, 4)
    gather1(1, 1)
    gather2(0, 3)
    gather3(0, 2)
    gather2(0, 4)
    gather1(1, 3)
    gather3(0, 0)
    gather3(0, 3)
    back_product(1)
    gather2(1, 0)
    back_product(2)
    gather3(0, 4)
    gather2(1, 3)
    scatter_x(1)
    scatter_x(2)
    gather2(1, 1)
    gather1(1, 4)
    back_product(3)
    gather1(1, 2)
    back_product(4)
    scatter_x(4)
    scatter_z(1)
    back_product(0)
    gather3(1, 0)
    scatter_z(2)
    scatter_x(3)
    gather3(1, 3)
    gather2(1, 2)
    grad_in(2)
    scatter_x(0)
    gather3(1, 1)
    scatter_z(4)
    grad_in(1)
    scatter_z(3)
    grad_in(0)
    partial_out(0)
    gather2(1, 4)
    gather3(1, 2)
    gather3(1, 4)
    scatter_z(0)
    partial_out(1)
    scaled = total_back()
    partial_out(2)
    partial_out(3)
    last_out()
    finish_input(scaled)

    for a in (0, 1):
        departed(("z", a), gath.at[a, pl.ds(0, 7), 0])
        departed(("k", a), gath.at[a, pl.ds(0, 7), 0])
        departed(("o", a), w_in.at[pl.ds(0, 96)])
        departed(("p", a), part.at[a, :, pl.ds(0, 256)])
        departed(("b", a), part.at[a, :, pl.ds(0, 256)])
        departed(("af", a), sa.at[a, pl.ds(0, 128)])
        departed(("a3", a), rbx.at[a])
        departed(("b3", a), rbx.at[a])
        departed(("g1", a), sb.at[a])
        departed(("h2", a), hid.at[a, :, pl.ds(0, 256)])
        departed(("g2", a), sa.at[a, pl.ds(0, 128)])
        departed(("g3", a), hid.at[a, :, pl.ds(0, 256)])
    departed(("n",), gs)
    departed(("x",), xs)
    departed(("s",), zs.at[pl.ds(1, 7)])
    departed(("st",), st.at[pl.ds(1, 7)])
    departed(("ft",), ft.at[pl.ds(1, 7)])


def deliver(*refs):
    sources, targets, sem = refs[:4], refs[4:8], refs[8]
    copies = [
        pltpu.make_async_copy(src, dst, sem.at[i])
        for i, (src, dst) in enumerate(zip(sources, targets))
    ]
    for copy in copies:
        copy.start()
    for copy in copies:
        copy.wait()


def local(inputs, gain, w_in, bias, w_out, cotangent):
    vmem = pl.BlockSpec(memory_space=pltpu.VMEM)
    anywhere = pl.BlockSpec(memory_space=pl.ANY)
    shapes = (
        jax.ShapeDtypeStruct((32, BLK), BF16),
        jax.ShapeDtypeStruct((BLK, BLK), BF16),
        jax.ShapeDtypeStruct((BLK,), F32),
        jax.ShapeDtypeStruct((BLK, BLK), BF16),
    )
    results = pl.pallas_call(
        kernel,
        out_shape=tuple(pltpu.VMEM(x.shape, x.dtype) for x in shapes),
        in_specs=[anywhere] * 6,
        out_specs=[vmem] * 4,
        scratch_shapes=[
            pltpu.VMEM((32, BLK), BF16),
            pltpu.VMEM((1, BLK), F32),
            pltpu.VMEM((BLK, BLK), BF16),
            pltpu.VMEM((1, BLK), F32),
            pltpu.VMEM((BLK, BLK), BF16),
            pltpu.VMEM((2, 8, 2, 64, BLK), BF16),
            pltpu.VMEM((2, TOKENS, BLK), BF16),
            pltpu.VMEM((2, TOKENS // 2, CA), BF16),
            pltpu.VMEM((2, TOKENS // 2, CA), BF16),
            pltpu.VMEM((2, 2, TOKENS // 8, HA), BF16),
            pltpu.VMEM((2, 2, TOKENS // 8, CA), BF16),
            pltpu.VMEM((2, 2, TOKENS // 4, HB), BF16),
            pltpu.VMEM((2, 2, TOKENS // 4, CB), BF16),
            pltpu.VMEM((2, TOKENS // 4, CB), BF16),
            pltpu.VMEM((2, TOKENS // 8, CB), BF16),
            pltpu.VMEM((2, TOKENS, BLK), BF16),
            pltpu.VMEM((8, 64, BLK), F32),
            pltpu.VMEM((8, 64, BLK), BF16),
            pltpu.VMEM((8, 64, BLK), BF16),
            pltpu.VMEM((8, 32, BLK), BF16),
            pltpu.VMEM((8, 32, BLK), BF16),
            pltpu.VMEM((8, 32, BLK), BF16),
            pltpu.VMEM((8, 32, BLK), BF16),
            pltpu.VMEM((BLK, BLK), F32),
            pltpu.VMEM((8, 8, 128), F32),
            pltpu.VMEM((8, 8, 128), F32),
            pltpu.SemaphoreType.DMA((6,)),
            pltpu.SemaphoreType.DMA((N_SEND,)),
            pltpu.SemaphoreType.DMA((N_RECV,)),
        ],
        compiler_params=pltpu.CompilerParams(
            collective_id=0, has_side_effects=True, vmem_limit_bytes=56 * 2**20
        ),
        name="mlp_backward",
    )(inputs, gain, w_in, bias, w_out, cotangent)
    return pl.pallas_call(
        deliver,
        out_shape=shapes,
        in_specs=[vmem] * 4,
        out_specs=[anywhere] * 4,
        scratch_shapes=[pltpu.SemaphoreType.DMA((4,))],
        compiler_params=pltpu.CompilerParams(vmem_limit_bytes=4 * 2**20),
        name="deliver",
    )(*results)


def solution(mesh):
    in_specs = (
        P("col", "row"),
        P("row"),
        P("row", "col"),
        P("col"),
        P("col", "row"),
        P("col", "row"),
    )
    out_specs = (P("col", "row"), P("row", "col"), P("col"), P("col", "row"))
    return jax.shard_map(local, mesh=mesh, in_specs=in_specs, out_specs=out_specs, check_vma=False)
```

```python
import functools

import jax
import jax.numpy as jnp
from jax import lax
from jax.experimental import pallas as pl
from jax.experimental.pallas import tpu as pltpu
from jax.sharding import PartitionSpec as P

MESH = pl.DeviceIdType.MESH
F32, BF16 = jnp.float32, jnp.bfloat16
D = 6144
EPS = 1e-06
TOKENS, BLK = 1024, 768
CA = 256
CB = BLK - CA
HA, HB = CA // 2, CB // 2
COLS_A, COLS_B = pl.ds(0, CA), pl.ds(CA, CB)
DELTA = (0, 1, -1, 2, -2, 3, -3, 4)
CHUNKS = ((0, 1), (1, 3), (3, 5), (5, 7), (7, 8))
LAST = len(CHUNKS) - 1
N_SEND, N_RECV = 40, 200


def normal_parts(pre_act):
    cumulative = 0.5 * (1.0 + lax.erf(pre_act * 0.7071067811865476))
    density = jnp.exp(-0.5 * pre_act * pre_act) * 0.3989422804014327
    return cumulative, density


def slot_of(delta):
    return DELTA.index(4 if delta in (4, -4) else delta)


def kernel(
    inp_hbm, gain_hbm, w_in_hbm, bias_hbm, w_out_hbm, cot_hbm, gi, gwi, gb, gwo,
    inp, gain, w_in, bias, w_out, gath, part, ra1, sa, raf, ra3, rbf, rb, sb, rbx, hid,
    gk, gs, gr, xs, xr, zs, zr, acc, st, ft, load_sem, send_sem, recv_sem,
):
    row, col = lax.axis_index("row"), lax.axis_index("col")
    y, xl = row // 2, row % 2
    xh, z, k = col // 16, (col // 2) % 8, col % 2

    def dev(dy=0, dx=0, dh=0, dz=0, dk=0):
        return (
            ((y + dy + 4) % 4) * 2 + (xl + dx) % 2,
            ((xh + dh) % 2) * 16 + ((z + dz + 8) % 8) * 2 + (k + dk) % 2,
        )

    xp, yp, ym, y2 = 1 - xl, (y + 1) % 4, (y + 3) % 4, (y + 2) % 4
    ROW_PEERS = [(dy, dx) for dy in range(4) for dx in range(2) if dy or dx]
    partners = [dev(dy=a, dx=b) for a, b in ROW_PEERS]
    partners += [dev(dz=1), dev(dz=-1), dev(dk=1), dev(dh=1), dev(dh=1, dk=1)]
    barrier = pltpu.get_barrier_semaphore()
    for partner in partners:
        pl.semaphore_signal(barrier, inc=1, device_id=partner, device_id_type=MESH)
    loads = [
        pltpu.make_async_copy(src, dst, load_sem.at[i])
        for i, (src, dst) in enumerate((
            (cot_hbm, gath.at[0, 0, 0, pl.ds(0, 32)]),
            (inp_hbm, inp),
            (gain_hbm, gain.at[0]),
            (bias_hbm, bias.at[0]),
            (w_out_hbm, w_out),
            (w_in_hbm, w_in),
        ))
    ]
    for load in loads:
        load.start()

    send_index, recv_index = {}, {}

    def send(key, kind, src, dst, to):
        pltpu.make_async_remote_copy(
            src_ref=src, dst_ref=dst,
            send_sem=send_sem.at[send_index.setdefault(kind, len(send_index))],
            recv_sem=recv_sem.at[recv_index.setdefault(key, len(recv_index))],
            device_id=to, device_id_type=MESH,
        ).start()

    def all_of(ref, kind, key):
        return pltpu.make_async_remote_copy(
            src_ref=ref, dst_ref=ref, send_sem=send_sem.at[send_index[kind]],
            recv_sem=recv_sem.at[recv_index[key]], device_id=dev(dk=1), device_id_type=MESH,
        )

    def arrived(key, ref):
        all_of(ref, ("st",), key).wait_recv()

    def departed(kind, ref):
        all_of(ref, kind, ("st",)).wait_send()

    lane = lax.broadcasted_iota(jnp.int32, (32, 128), 1)

    def pair(a, b):
        columns = jnp.where(lane < 64, a, b)
        return jnp.concatenate([columns, jnp.zeros((96, 128), F32)], 0).T[60:68]

    loads[0].wait()
    loads[1].wait()
    values = inp[...].astype(F32)
    st[0] = pair(
        jnp.sum(values, 1, keepdims=True), jnp.sum(values * values, 1, keepdims=True)
    )
    pl.semaphore_wait(barrier, len(partners))

    def all_row(tag, ref):
        for i, (dy, dx) in enumerate(ROW_PEERS):
            send((tag,), (tag,), ref.at[0], ref.at[i + 1], dev(dy=dy, dx=dx))

    def row_sum(tag, ref):
        arrived((tag,), ref.at[pl.ds(1, 7)])
        total = ref[0]
        for i in range(1, 8):
            total = total + ref[i]
        columns = jnp.concatenate([total, jnp.zeros((120, 128), F32)], 0).T
        return columns[0:32, 0:1] * (1.0 / D), columns[0:32, 4:5] * (1.0 / D)

    def unit(a, slot, u):
        return gath.at[a, slot, 0, pl.ds(u * 32, 32)]

    def pass_z(a, u, origin, slot, dz):
        send(("z", a, u, slot), ("z", a), unit(a, origin, u), unit(a, slot, u), dev(dz=dz))

    def z_first(a, u):
        pass_z(a, u, 0, 2, 1)
        pass_z(a, u, 0, 1, -1)

    def to_sibling(a, h, slot, u):
        mine = unit(a, slot, u)
        send(("k", a, min(h, LAST)), ("k", a), mine, gath.at[a, slot, 1, pl.ds(u * 32, 32)], dev(dk=1))

    def own(a):
        mine = unit(a, 0, 0)
        send(("h", a), ("o", a), mine, unit(a, 0, 1), dev(dh=1))
        z_first(a, 0)
        send(("k", a, 0), ("o", a), mine, gath.at[a, 0, 1, pl.ds(32, 32)], dev(dh=1, dk=1))
        send(("k", a, 0), ("o", a), mine, gath.at[a, 0, 1, pl.ds(0, 32)], dev(dk=1))

    def other(a):
        arrived(("h", a), unit(a, 0, 1))
        z_first(a, 1)

    def hop(a, u, h):
        if h == 4:
            arrived(("z", a, u, 7), unit(a, 7, u))
            to_sibling(a, h, 7, u)
            return
        for slot, dz in ((slot_of(-h), 1), (slot_of(h), -1)):
            arrived(("z", a, u, slot), unit(a, slot, u))
            if h < 3 or u == (dz < 0):
                pass_z(a, u, slot, slot_of(-dz * (h + 1)), dz)
            to_sibling(a, h, slot, u)

    def span(c):
        s0, s1 = CHUNKS[c]
        return s0 * 128, (s1 - s0) * 128

    def at(base, index, size):
        return pl.ds(pl.multiple_of(base + index * size, 16), size)

    def product(a, c):
        off, t = span(c)
        s0, s1 = CHUNKS[c]
        arrived(("k", a, c), gath.at[a, pl.ds(s0, s1 - s0), 1])
        rows = gath[a, s0:s1].reshape(t, BLK)
        if a == 0:
            out = lax.dot_general(
                rows, w_out[...], (((1,), (1,)), ((), ())), preferred_element_type=F32
            )
        else:
            out = jnp.dot(rows, w_in[...], preferred_element_type=F32)
        part[a, off:off + t, :] = out.astype(BF16)
        far = at(off, y2, t // 4)
        quarter = pl.ds(off // 4, t // 4)
        for i, dy in ((0, 1), (1, -1)):
            send(
                ("bf", a, c), ("p", a), part.at[a, far, pl.ds(CA + i * HB, HB)],
                rbf.at[a, i, quarter], dev(dy=dy),
            )
        send(
            ("a1", a, c), ("p", a), part.at[a, at(off, xp, t // 2), COLS_A],
            ra1.at[a, pl.ds(off // 2, t // 2)], dev(dx=1),
        )

    def merge(ref, a, rows, cols, other):
        ref[a, rows, cols] = (ref[a, rows, cols].astype(F32) + other.astype(F32)).astype(BF16)

    def reduce2_b(a, c):
        off, t = span(c)
        o4, t4 = off // 4, t // 4
        arrived(("bf", a, c), rbf.at[a, :, pl.ds(o4, t4)])
        for i, block, start, dy in ((0, yp, CA, 1), (1, ym, CA + HB, -1)):
            merge(part, a, at(off, block, t4), pl.ds(start, HB), rbf[a, i, o4:o4 + t4])
            send(
                ("b", a, c), ("b", a), part.at[a, at(off, block, t4), COLS_B],
                rb.at[a, i, pl.ds(o4, t4)], dev(dy=dy),
            )

    def reduce2_a(a, c):
        off, t = span(c)
        o2, o8, t2, t8 = off // 2, off // 8, t // 2, t // 8
        arrived(("a1", a, c), ra1.at[a, pl.ds(o2, t2)])
        total = part[a, at(off, xl, t2), COLS_A].astype(F32) + ra1[a, o2:o2 + t2].astype(F32)
        sa[a, o2:o2 + t2] = total.astype(BF16)
        for i, dy in ((0, 1), (1, -1)):
            send(
                ("af", a, c), ("af", a), sa.at[a, at(o2, y2, t8), pl.ds(i * HA, HA)],
                raf.at[a, i, pl.ds(o8, t8)], dev(dy=dy),
            )

    def reduce3_a(a, c):
        off, t = span(c)
        o2, o8, t8 = off // 2, off // 8, t // 8
        arrived(("af", a, c), raf.at[a, :, pl.ds(o8, t8)])
        for i, block, start, dy in ((0, yp, 0, 1), (1, ym, HA, -1)):
            merge(sa, a, at(o2, block, t8), pl.ds(start, HA), raf[a, i, o8:o8 + t8])
            send(
                ("a3", a, c), ("a3", a), sa.at[a, at(o2, block, t8)],
                ra3.at[a, i, pl.ds(o8, t8)], dev(dy=dy),
            )

    def reduce3_b(a, c):
        off, t = span(c)
        o4, o8, t4, t8 = off // 4, off // 8, t // 4, t // 8
        arrived(("b", a, c), rb.at[a, :, pl.ds(o4, t4)])
        total = part[a, at(off, y, t4), COLS_B].astype(F32)
        for i in (0, 1):
            total = total + rb[a, i, o4:o4 + t4].astype(F32)
        sb[a, o4:o4 + t4] = total.astype(BF16)
        send(
            ("b3", a, c), ("b3", a), sb.at[a, at(o4, xp, t8)], rbx.at[a, pl.ds(o8, t8)],
            dev(dx=1),
        )

    def rows_a(c):
        off, t = span(c)
        return at(off, xl * 4 + y, t // 8)

    def rows_b(c):
        off, t = span(c)
        return at(off, y * 2 + xl, t // 8)

    def finish(rows, cols, bias_part, totals):
        pre_act = totals[1] + bias_part
        cumulative, density = normal_parts(pre_act)
        hid[0, rows, cols] = (totals[0] * (cumulative + pre_act * density)).astype(BF16)
        hid[1, rows, cols] = (pre_act * cumulative).astype(BF16)

    def elementwise_a(c):
        off, t = span(c)
        o2, o8, t8 = off // 2, off // 8, t // 8
        totals = []
        for a in (0, 1):
            arrived(("a3", a, c), ra3.at[a, :, pl.ds(o8, t8)])
            total = sa[a, at(o2, y, t8)].astype(F32)
            for i in (0, 1):
                total = total + ra3[a, i, o8:o8 + t8].astype(F32)
            totals.append(total)
        finish(rows_a(c), COLS_A, bias[:, 0:CA], totals)

    def elementwise_b(c):
        off, t = span(c)
        o4, o8, t8 = off // 4, off // 8, t // 8
        totals = []
        for a in (0, 1):
            arrived(("b3", a, c), rbx.at[a, pl.ds(o8, t8)])
            totals.append(sb[a, at(o4, xl, t8)].astype(F32) + rbx[a, o8:o8 + t8].astype(F32))
        finish(rows_b(c), COLS_B, bias[:, CA:BLK], totals)

    def share(key, kind, ref, to):
        send(key, kind, ref, ref, to)

    def block_a(g, c, index, cols=COLS_A):
        off, t = span(c)
        return hid.at[g, at(off, xl * 4 + index, t // 8), cols]

    def block_b(g, c, index, cols=COLS_B):
        off, t = span(c)
        return hid.at[g, at(off, index, t // 4), cols]

    def gather1_b(g, c):
        share(("h1", g, c), ("h1", g), hid.at[g, rows_b(c), COLS_B], dev(dx=1))

    def gather1_a(g, c):
        for i, dy in ((0, 1), (1, -1)):
            share(("g1", g, c, i), ("g1", g), block_a(g, c, y), dev(dy=dy))

    def gather2_b(g, c):
        off, t = span(c)
        arrived(("h1", g, c), hid.at[g, at(off, y * 2 + xp, t // 8), COLS_B])
        for i, dy in ((0, 1), (1, -1)):
            share(("h2", g, c, i), ("h2", g), block_b(g, c, y), dev(dy=dy))

    def gather2_a(g, c):
        for i, block, dy in ((0, ym, 1), (1, yp, -1)):
            arrived(("g1", g, c, i), block_a(g, c, block))
            share(("g2", g, c), ("g2", g), block_a(g, c, block, pl.ds(i * HA, HA)), dev(dy=dy))

    def gather3_b(g, c):
        for i, block, dy in ((0, ym, 1), (1, yp, -1)):
            arrived(("h2", g, c, i), block_b(g, c, block))
            share(("h3", g, c), ("h3", g), block_b(g, c, block, pl.ds(CA + i * HB, HB)), dev(dy=dy))

    def gather3_a(g, c):
        off, t = span(c)
        arrived(("g2", g, c), block_a(g, c, y2))
        share(("g3", g, c), ("g3", g), hid.at[g, at(off, xl, t // 2), COLS_A], dev(dx=1))

    def gathered(g, c):
        off, t = span(c)
        arrived(("g3", g, c), hid.at[g, at(off, xp, t // 2), COLS_A])
        arrived(("h3", g, c), block_b(g, c, y2))

    ready = set()

    def all_gathered(g, chunks):
        for c in chunks:
            if (g, c) not in ready:
                ready.add((g, c))
                gathered(g, c)

    def back_product(c):
        all_gathered(0, (c,))
        off, t = span(c)
        s0, s1 = CHUNKS[c]
        out = lax.dot_general(
            hid[0, off:off + t, :], w_in[...], (((1,), (1,)), ((), ())),
            preferred_element_type=F32,
        )
        for slot in range(s0, s1):
            base = (slot - s0) * 128
            gk[slot] = out[base:base + 64]
            gs[slot] = out[base + 64:base + 128].astype(BF16)
        send(("n", c), ("n",), gs.at[pl.ds(s0, s1 - s0)], gr.at[pl.ds(s0, s1 - s0)], dev(dk=1))

    def scatter_x(c):
        s0, s1 = CHUNKS[c]
        arrived(("n", c), gr.at[pl.ds(s0, s1 - s0)])
        for slot in range(s0, s1):
            total = gk[slot] + gr[slot].astype(F32)
            gk[slot, 0:32] = total[0:32]
            xs[slot] = total[32:64].astype(BF16)
        send(("x", c), ("x",), xs.at[pl.ds(s0, s1 - s0)], xr.at[pl.ds(s0, s1 - s0)], dev(dh=1))

    def scatter_z(c):
        s0, s1 = CHUNKS[c]
        arrived(("x", c), xr.at[pl.ds(s0, s1 - s0)])
        for slot in range(s0, s1):
            total = gk[slot, 0:32] + xr[slot].astype(F32)
            if slot == 0:
                gk[0, 0:32] = total
            else:
                zs[slot] = total.astype(BF16)
                send(("s",), ("s",), zs.at[slot], zr.at[slot], dev(dz=DELTA[slot]))

    scale = float(TOKENS) ** (-0.5)
    tiles = [(i * 256, (i + 1) * 256) for i in range(3)]

    def outer(left, right):
        return lax.dot_general(
            left, right, (((0,), (0,)), ((), ())), preferred_element_type=F32
        )

    def flat(a, s0=0, s1=8):
        return gath[a, s0:s1].reshape((s1 - s0) * 128, BLK)

    def grad_in(n):
        all_gathered(0, range(LAST + 1))
        i, j = tiles[n]
        gwi[i:j, :] = (outer(flat(1)[:, i:j], hid[0]) * scale).astype(BF16)
        if n == 0:
            gb[...] = (jnp.sum(hid[0].astype(F32), 0, keepdims=True) * scale).reshape(BLK)

    def total_back():
        total = gk[0, 0:32]
        arrived(("s",), zr.at[pl.ds(1, 7)])
        for slot in range(1, 8):
            total = total + zr[slot].astype(F32)
        scaled = total * gain[...]
        ft[0] = pair(
            jnp.sum(scaled, 1, keepdims=True), jnp.sum(scaled * centred, 1, keepdims=True)
        )
        all_row("ft", ft)
        return scaled

    def finish_input(scaled):
        first, cross = row_sum("ft", ft)
        gi[...] = (inv_std * (scaled - first - centred * cross)).astype(BF16)

    def rows_out(c, i, j):
        s0, s1 = CHUNKS[c]
        return outer(hid[1, s0 * 128:s1 * 128, i:j], flat(0, s0, s1))

    def partial_out(c):
        all_gathered(1, (c,))
        for i, j in tiles:
            acc[i:j, :] = acc[i:j, :] + rows_out(c, i, j) if c else rows_out(c, i, j)

    def last_out():
        all_gathered(1, (LAST,))
        for i, j in tiles:
            gwo[i:j, :] = ((acc[i:j, :] + rows_out(LAST, i, j)) * scale).astype(BF16)

    own(0)
    all_row("st", st)
    mean_x, second = row_sum("st", st)
    inv_std = lax.rsqrt(second - mean_x * mean_x + EPS)
    centred = (values - mean_x) * inv_std
    loads[2].wait()
    gath[1, 0, 0, 0:32] = (centred * gain[...]).astype(BF16)
    own(1)
    other(0)
    loads[4].wait()
    product(0, 0)
    hop(0, 0, 1)
    other(1)
    loads[5].wait()
    product(1, 0)
    hop(0, 1, 1)
    hop(1, 0, 1)
    reduce2_a(0, 0)
    reduce2_b(0, 0)
    product(0, 1)
    hop(1, 1, 1)
    reduce2_b(1, 0)
    hop(0, 0, 2)
    reduce3_a(0, 0)
    reduce2_a(1, 0)
    product(1, 1)
    hop(0, 1, 2)
    reduce2_b(0, 1)
    hop(1, 0, 2)
    reduce2_a(0, 1)
    product(0, 2)
    reduce3_b(1, 0)
    hop(1, 1, 2)
    reduce3_a(1, 0)
    reduce2_b(1, 1)
    product(1, 2)
    hop(0, 0, 3)
    reduce3_a(0, 1)
    hop(0, 1, 3)
    reduce2_a(1, 1)
    hop(1, 0, 3)
    reduce3_b(0, 1)
    reduce3_b(0, 0)
    reduce2_b(0, 2)
    hop(1, 1, 3)
    product(0, 3)
    reduce2_a(0, 2)
    reduce2_a(1, 2)
    hop(0, 0, 4)
    reduce2_b(1, 2)
    hop(0, 1, 4)
    product(1, 3)
    reduce3_b(1, 1)
    reduce3_a(1, 1)
    hop(1, 1, 4)
    product(0, 4)
    reduce2_b(0, 3)
    reduce3_a(1, 2)
    hop(1, 0, 4)
    reduce3_b(0, 2)
    loads[3].wait()
    elementwise_a(0)
    reduce3_a(0, 2)
    product(1, 4)
    reduce3_b(1, 2)
    reduce2_b(1, 3)
    reduce2_a(0, 3)
    reduce2_a(1, 3)
    elementwise_b(1)
    gather1_a(0, 0)
    reduce2_b(0, 4)
    gather1_b(0, 1)
    reduce3_b(0, 3)
    reduce2_a(0, 4)
    elementwise_a(2)
    elementwise_b(0)
    gather1_b(0, 0)
    reduce2_b(1, 4)
    elementwise_a(1)
    reduce2_a(1, 4)
    gather1_a(0, 2)
    elementwise_b(2)
    gather1_a(0, 1)
    gather1_b(0, 2)
    reduce3_b(1, 3)
    gather1_b(1, 0)
    reduce3_a(0, 3)
    reduce3_a(1, 3)
    gather1_b(1, 1)
    gather2_a(0, 0)
    gather2_b(0, 1)
    reduce3_b(0, 4)
    reduce3_a(0, 4)
    reduce3_a(1, 4)
    reduce3_b(1, 4)
    gather2_a(0, 1)
    gather2_a(0, 2)
    elementwise_b(3)
    gather1_b(0, 3)
    elementwise_a(3)
    gather1_a(0, 3)
    gather3_a(0, 0)
    gather1_b(1, 2)
    gather2_b(0, 2)
    gather3_b(0, 1)
    elementwise_b(4)
    elementwise_a(4)
    gather1_b(0, 4)
    gather1_a(0, 4)
    gather3_a(0, 1)
    gather3_a(0, 2)
    gather2_a(0, 3)
    gather2_b(0, 3)
    gather3_b(0, 2)
    gather2_a(0, 4)
    gather2_b(0, 4)
    gather2_b(0, 0)
    gather3_a(0, 3)
    back_product(1)
    gather3_b(0, 3)
    gather1_a(1, 1)
    gather1_a(1, 3)
    gather3_a(0, 4)
    back_product(2)
    scatter_x(1)
    gather3_b(0, 4)
    gather1_a(1, 0)
    scatter_x(2)
    gather1_b(1, 4)
    gather3_b(0, 0)
    gather2_b(1, 0)
    back_product(3)
    gather1_b(1, 3)
    gather2_a(1, 1)
    back_product(4)
    gather1_a(1, 2)
    gather2_a(1, 0)
    gather2_a(1, 3)
    gather2_b(1, 2)
    scatter_x(4)
    scatter_z(1)
    scatter_x(3)
    gather1_a(1, 4)
    back_product(0)
    scatter_z(2)
    gather2_b(1, 4)
    gather2_b(1, 1)
    grad_in(2)
    gather3_a(1, 1)
    grad_in(0)
    gather3_a(1, 0)
    gather2_a(1, 2)
    gather3_b(1, 0)
    scatter_z(4)
    gather3_a(1, 3)
    gather2_a(1, 4)
    gather2_b(1, 3)
    scatter_x(0)
    scatter_z(3)
    gather3_b(1, 1)
    partial_out(0)
    gather3_a(1, 2)
    gather3_b(1, 2)
    gather3_b(1, 3)
    gather3_b(1, 4)
    scatter_z(0)
    gather3_a(1, 4)
    grad_in(1)
    partial_out(1)
    scaled = total_back()
    partial_out(2)
    partial_out(3)
    last_out()
    finish_input(scaled)

    for a in (0, 1):
        departed(("z", a), gath.at[a, pl.ds(0, 7), 0])
        departed(("k", a), gath.at[a, pl.ds(0, 7), 0])
        departed(("o", a), w_in.at[pl.ds(0, 96)])
        departed(("p", a), part.at[a, :, pl.ds(0, 256)])
        departed(("b", a), part.at[a, :, pl.ds(0, 256)])
        departed(("af", a), sa.at[a, pl.ds(0, 128)])
        departed(("a3", a), rbx.at[a])
        departed(("b3", a), rbx.at[a])
        departed(("g1", a), rbx.at[a])
        departed(("h1", a), rbx.at[a])
        departed(("h2", a), hid.at[a, :, pl.ds(0, 256)])
        departed(("g2", a), sa.at[a, pl.ds(0, 128)])
        departed(("g3", a), sa.at[a])
        departed(("h3", a), sb.at[a])
    departed(("n",), gs)
    departed(("x",), xs)
    departed(("s",), zs.at[pl.ds(1, 7)])
    departed(("st",), st.at[pl.ds(1, 7)])
    departed(("ft",), ft.at[pl.ds(1, 7)])


def deliver(*refs):
    sources, targets, sem = refs[:4], refs[4:8], refs[8]
    copies = [
        pltpu.make_async_copy(src, dst, sem.at[i])
        for i, (src, dst) in enumerate(zip(sources, targets))
    ]
    for copy in copies:
        copy.start()
    for copy in copies:
        copy.wait()


def local(inputs, gain, w_in, bias, w_out, cotangent):
    vmem = pl.BlockSpec(memory_space=pltpu.VMEM)
    anywhere = pl.BlockSpec(memory_space=pl.ANY)
    shapes = (
        jax.ShapeDtypeStruct((32, BLK), BF16),
        jax.ShapeDtypeStruct((BLK, BLK), BF16),
        jax.ShapeDtypeStruct((BLK,), F32),
        jax.ShapeDtypeStruct((BLK, BLK), BF16),
    )
    results = pl.pallas_call(
        kernel,
        out_shape=tuple(pltpu.VMEM(x.shape, x.dtype) for x in shapes),
        in_specs=[anywhere] * 6,
        out_specs=[vmem] * 4,
        scratch_shapes=[
            pltpu.VMEM((32, BLK), BF16),
            pltpu.VMEM((1, BLK), F32),
            pltpu.VMEM((BLK, BLK), BF16),
            pltpu.VMEM((1, BLK), F32),
            pltpu.VMEM((BLK, BLK), BF16),
            pltpu.VMEM((2, 8, 2, 64, BLK), BF16),
            pltpu.VMEM((2, TOKENS, BLK), BF16),
            pltpu.VMEM((2, TOKENS // 2, CA), BF16),
            pltpu.VMEM((2, TOKENS // 2, CA), BF16),
            pltpu.VMEM((2, 2, TOKENS // 8, HA), BF16),
            pltpu.VMEM((2, 2, TOKENS // 8, CA), BF16),
            pltpu.VMEM((2, 2, TOKENS // 4, HB), BF16),
            pltpu.VMEM((2, 2, TOKENS // 4, CB), BF16),
            pltpu.VMEM((2, TOKENS // 4, CB), BF16),
            pltpu.VMEM((2, TOKENS // 8, CB), BF16),
            pltpu.VMEM((2, TOKENS, BLK), BF16),
            pltpu.VMEM((8, 64, BLK), F32),
            pltpu.VMEM((8, 64, BLK), BF16),
            pltpu.VMEM((8, 64, BLK), BF16),
            pltpu.VMEM((8, 32, BLK), BF16),
            pltpu.VMEM((8, 32, BLK), BF16),
            pltpu.VMEM((8, 32, BLK), BF16),
            pltpu.VMEM((8, 32, BLK), BF16),
            pltpu.VMEM((BLK, BLK), F32),
            pltpu.VMEM((8, 8, 128), F32),
            pltpu.VMEM((8, 8, 128), F32),
            pltpu.SemaphoreType.DMA((6,)),
            pltpu.SemaphoreType.DMA((N_SEND,)),
            pltpu.SemaphoreType.DMA((N_RECV,)),
        ],
        compiler_params=pltpu.CompilerParams(
            collective_id=0, has_side_effects=True, vmem_limit_bytes=56 * 2**20
        ),
        name="mlp_backward",
    )(inputs, gain, w_in, bias, w_out, cotangent)
    return pl.pallas_call(
        deliver,
        out_shape=shapes,
        in_specs=[vmem] * 4,
        out_specs=[anywhere] * 4,
        scratch_shapes=[pltpu.SemaphoreType.DMA((4,))],
        compiler_params=pltpu.CompilerParams(vmem_limit_bytes=4 * 2**20),
        name="deliver",
    )(*results)


def solution(mesh):
    in_specs = (
        P("col", "row"),
        P("row"),
        P("row", "col"),
        P("col"),
        P("col", "row"),
        P("col", "row"),
    )
    out_specs = (P("col", "row"), P("row", "col"), P("col"), P("col", "row"))
    return jax.shard_map(local, mesh=mesh, in_specs=in_specs, out_specs=out_specs, check_vma=False)
```

```python
import functools

import jax
import jax.numpy as jnp
from jax import lax
from jax.experimental import pallas as pl
from jax.experimental.pallas import tpu as pltpu
from jax.sharding import PartitionSpec as P

MESH = pl.DeviceIdType.MESH
F32, BF16 = jnp.float32, jnp.bfloat16
D = 6144
EPS = 1e-06
TOKENS, BLK = 1024, 768
CA = 256
CB = BLK - CA
HA, HB = CA // 2, CB // 2
COLS_A, COLS_B = pl.ds(0, CA), pl.ds(CA, CB)
DELTA = (0, 1, -1, 2, -2, 3, -3, 4)
CHUNKS = ((0, 1), (1, 3), (3, 5), (5, 7), (7, 8))
LAST = len(CHUNKS) - 1
N_SEND, N_RECV = 33, 140


def normal_parts(pre_act):
    cumulative = 0.5 * (1.0 + lax.erf(pre_act * 0.7071067811865476))
    density = jnp.exp(-0.5 * pre_act * pre_act) * 0.3989422804014327
    return cumulative, density


def slot_of(delta):
    return DELTA.index(4 if delta in (4, -4) else delta)


def kernel(
    inp_hbm, gain_hbm, w_in_hbm, bias_hbm, w_out_hbm, cot_hbm, gi, gwi, gb, gwo,
    inp, gain, w_in, bias, w_out, gath, part, ra1, sa, raf, ra3, rbf, rb, sb, rbx, hid,
    gk, gs, gr, xs, xr, zs, zr, acc, st, ft, load_sem, send_sem, recv_sem,
):
    row, col = lax.axis_index("row"), lax.axis_index("col")
    y, xl = row // 2, row % 2
    xh, z, k = col // 16, (col // 2) % 8, col % 2

    def dev(dy=0, dx=0, dh=0, dz=0, dk=0):
        return (
            ((y + dy + 4) % 4) * 2 + (xl + dx) % 2,
            ((xh + dh) % 2) * 16 + ((z + dz + 8) % 8) * 2 + (k + dk) % 2,
        )

    xp, yp, ym, y2 = 1 - xl, (y + 1) % 4, (y + 3) % 4, (y + 2) % 4
    ROW_PEERS = [(dy, dx) for dy in range(4) for dx in range(2) if dy or dx]
    partners = [dev(dy=a, dx=b) for a, b in ROW_PEERS]
    partners += [dev(dz=1), dev(dz=-1), dev(dk=1), dev(dh=1), dev(dh=1, dk=1)]
    barrier = pltpu.get_barrier_semaphore()
    for partner in partners:
        pl.semaphore_signal(barrier, inc=1, device_id=partner, device_id_type=MESH)
    loads = [
        pltpu.make_async_copy(src, dst, load_sem.at[i])
        for i, (src, dst) in enumerate((
            (cot_hbm, gath.at[0, 0, 0, pl.ds(0, 32)]),
            (inp_hbm, inp),
            (gain_hbm, gain.at[0]),
            (bias_hbm, bias.at[0]),
            (w_out_hbm, w_out),
            (w_in_hbm, w_in),
        ))
    ]
    for load in loads:
        load.start()

    send_index, recv_index = {}, {}

    def slot_key(key):
        kind, c = key[0], key[2] if len(key) > 2 else 0
        if kind == "h1":
            return ("bf",) + key[1:]
        if kind == "g1":
            return ("a1" if key[3] == 0 else "af", key[1], c)
        if kind == "h2" and c > 0:
            return ("z", key[1], key[3], 7 if c == LAST else 2 * c)
        if kind in ("g2", "h3") and 0 < c < LAST:
            return ("z", key[1], 0 if kind == "g2" else 1, 2 * c - 1)
        return key

    def send(key, kind, src, dst, to):
        pltpu.make_async_remote_copy(
            src_ref=src, dst_ref=dst,
            send_sem=send_sem.at[send_index.setdefault(kind, len(send_index))],
            recv_sem=recv_sem.at[recv_index.setdefault(slot_key(key), len(recv_index))],
            device_id=to, device_id_type=MESH,
        ).start()

    def all_of(ref, kind, key):
        return pltpu.make_async_remote_copy(
            src_ref=ref, dst_ref=ref, send_sem=send_sem.at[send_index[kind]],
            recv_sem=recv_sem.at[recv_index[slot_key(key)]], device_id=dev(dk=1), device_id_type=MESH,
        )

    def arrived(key, ref):
        all_of(ref, ("st",), key).wait_recv()

    def departed(kind, ref):
        all_of(ref, kind, ("st",)).wait_send()

    lane = lax.broadcasted_iota(jnp.int32, (32, 128), 1)

    def pair(a, b):
        columns = jnp.where(lane < 64, a, b)
        return jnp.concatenate([columns, jnp.zeros((96, 128), F32)], 0).T[60:68]

    loads[0].wait()
    loads[1].wait()
    values = inp[...].astype(F32)
    st[0] = pair(
        jnp.sum(values, 1, keepdims=True), jnp.sum(values * values, 1, keepdims=True)
    )
    pl.semaphore_wait(barrier, len(partners))

    def all_row(tag, ref):
        for i, (dy, dx) in enumerate(ROW_PEERS):
            send((tag,), (tag,), ref.at[0], ref.at[i + 1], dev(dy=dy, dx=dx))

    def row_sum(tag, ref):
        arrived((tag,), ref.at[pl.ds(1, 7)])
        total = ref[0]
        for i in range(1, 8):
            total = total + ref[i]
        columns = jnp.concatenate([total, jnp.zeros((120, 128), F32)], 0).T
        return columns[0:32, 0:1] * (1.0 / D), columns[0:32, 4:5] * (1.0 / D)

    def unit(a, slot, u):
        return gath.at[a, slot, 0, pl.ds(u * 32, 32)]

    def pass_z(a, u, origin, slot, dz):
        send(("z", a, u, slot), ("z", a), unit(a, origin, u), unit(a, slot, u), dev(dz=dz))

    def z_first(a, u):
        pass_z(a, u, 0, 2, 1)
        pass_z(a, u, 0, 1, -1)

    def to_sibling(a, h, slot, u):
        mine = unit(a, slot, u)
        send(("k", a, min(h, LAST)), ("k", a), mine, gath.at[a, slot, 1, pl.ds(u * 32, 32)], dev(dk=1))

    def own(a):
        mine = unit(a, 0, 0)
        send(("h", a), ("o", a), mine, unit(a, 0, 1), dev(dh=1))
        z_first(a, 0)
        if a == 0:
            send(("k", a, 0), ("o", a), mine, gath.at[a, 0, 1, pl.ds(32, 32)], dev(dh=1, dk=1))
        send(("k", a, 0), ("o", a), mine, gath.at[a, 0, 1, pl.ds(0, 32)], dev(dk=1))

    def other(a):
        arrived(("h", a), unit(a, 0, 1))
        z_first(a, 1)
        if a == 1:
            send(("k", a, 0), ("o", a), unit(a, 0, 1), gath.at[a, 0, 1, pl.ds(32, 32)], dev(dk=1))

    def hop(a, u, h):
        if h == 4:
            arrived(("z", a, u, 7), unit(a, 7, u))
            to_sibling(a, h, 7, u)
            return
        for slot, dz in ((slot_of(-h), 1), (slot_of(h), -1)):
            arrived(("z", a, u, slot), unit(a, slot, u))
            if h < 3 or u == (dz < 0):
                pass_z(a, u, slot, slot_of(-dz * (h + 1)), dz)
            to_sibling(a, h, slot, u)

    def span(c):
        s0, s1 = CHUNKS[c]
        return s0 * 128, (s1 - s0) * 128

    def at(base, index, size):
        return pl.ds(pl.multiple_of(base + index * size, 16), size)

    def product(a, c):
        off, t = span(c)
        s0, s1 = CHUNKS[c]
        arrived(("k", a, c), gath.at[a, pl.ds(s0, s1 - s0), 1])
        rows = gath[a, s0:s1].reshape(t, BLK)
        if a == 0:
            out = lax.dot_general(
                rows, w_out[...], (((1,), (1,)), ((), ())), preferred_element_type=F32
            )
        else:
            out = jnp.dot(rows, w_in[...], preferred_element_type=F32)
        part[a, off:off + t, :] = out.astype(BF16)
        far = at(off, y2, t // 4)
        quarter = pl.ds(off // 4, t // 4)
        for i, dy in ((0, 1), (1, -1)):
            send(
                ("bf", a, c), ("p", a), part.at[a, far, pl.ds(CA + i * HB, HB)],
                rbf.at[a, i, quarter], dev(dy=dy),
            )
        send(
            ("a1", a, c), ("p", a), part.at[a, at(off, xp, t // 2), COLS_A],
            ra1.at[a, pl.ds(off // 2, t // 2)], dev(dx=1),
        )

    def merge(ref, a, rows, cols, other):
        ref[a, rows, cols] = (ref[a, rows, cols].astype(F32) + other.astype(F32)).astype(BF16)

    def reduce2_b(a, c):
        off, t = span(c)
        o4, t4 = off // 4, t // 4
        arrived(("bf", a, c), rbf.at[a, :, pl.ds(o4, t4)])
        for i, block, start, dy in ((0, yp, CA, 1), (1, ym, CA + HB, -1)):
            merge(part, a, at(off, block, t4), pl.ds(start, HB), rbf[a, i, o4:o4 + t4])
            send(
                ("b", a, c), ("b", a), part.at[a, at(off, block, t4), COLS_B],
                rb.at[a, i, pl.ds(o4, t4)], dev(dy=dy),
            )

    def reduce2_a(a, c):
        off, t = span(c)
        o2, o8, t2, t8 = off // 2, off // 8, t // 2, t // 8
        arrived(("a1", a, c), ra1.at[a, pl.ds(o2, t2)])
        total = part[a, at(off, xl, t2), COLS_A].astype(F32) + ra1[a, o2:o2 + t2].astype(F32)
        sa[a, o2:o2 + t2] = total.astype(BF16)
        for i, dy in ((0, 1), (1, -1)):
            send(
                ("af", a, c), ("af", a), sa.at[a, at(o2, y2, t8), pl.ds(i * HA, HA)],
                raf.at[a, i, pl.ds(o8, t8)], dev(dy=dy),
            )

    def reduce3_a(a, c):
        off, t = span(c)
        o2, o8, t8 = off // 2, off // 8, t // 8
        arrived(("af", a, c), raf.at[a, :, pl.ds(o8, t8)])
        for i, block, start, dy in ((0, yp, 0, 1), (1, ym, HA, -1)):
            merge(sa, a, at(o2, block, t8), pl.ds(start, HA), raf[a, i, o8:o8 + t8])
            send(
                ("a3", a, c), ("a3", a), sa.at[a, at(o2, block, t8)],
                ra3.at[a, i, pl.ds(o8, t8)], dev(dy=dy),
            )

    def reduce3_b(a, c):
        off, t = span(c)
        o4, o8, t4, t8 = off // 4, off // 8, t // 4, t // 8
        arrived(("b", a, c), rb.at[a, :, pl.ds(o4, t4)])
        total = part[a, at(off, y, t4), COLS_B].astype(F32)
        for i in (0, 1):
            total = total + rb[a, i, o4:o4 + t4].astype(F32)
        sb[a, o4:o4 + t4] = total.astype(BF16)
        send(
            ("b3", a, c), ("b3", a), sb.at[a, at(o4, xp, t8)], rbx.at[a, pl.ds(o8, t8)],
            dev(dx=1),
        )

    def rows_a(c):
        off, t = span(c)
        return at(off, xl * 4 + y, t // 8)

    def rows_b(c):
        off, t = span(c)
        return at(off, y * 2 + xl, t // 8)

    def finish(rows, cols, bias_part, totals):
        pre_act = totals[1] + bias_part
        cumulative, density = normal_parts(pre_act)
        hid[0, rows, cols] = (totals[0] * (cumulative + pre_act * density)).astype(BF16)
        hid[1, rows, cols] = (pre_act * cumulative).astype(BF16)

    def elementwise_a(c):
        off, t = span(c)
        o2, o8, t8 = off // 2, off // 8, t // 8
        totals = []
        for a in (0, 1):
            arrived(("a3", a, c), ra3.at[a, :, pl.ds(o8, t8)])
            total = sa[a, at(o2, y, t8)].astype(F32)
            for i in (0, 1):
                total = total + ra3[a, i, o8:o8 + t8].astype(F32)
            totals.append(total)
        finish(rows_a(c), COLS_A, bias[:, 0:CA], totals)

    def elementwise_b(c):
        off, t = span(c)
        o4, o8, t8 = off // 4, off // 8, t // 8
        totals = []
        for a in (0, 1):
            arrived(("b3", a, c), rbx.at[a, pl.ds(o8, t8)])
            totals.append(sb[a, at(o4, xl, t8)].astype(F32) + rbx[a, o8:o8 + t8].astype(F32))
        finish(rows_b(c), COLS_B, bias[:, CA:BLK], totals)

    def share(key, kind, ref, to):
        send(key, kind, ref, ref, to)

    def block_a(g, c, index, cols=COLS_A):
        off, t = span(c)
        return hid.at[g, at(off, xl * 4 + index, t // 8), cols]

    def block_b(g, c, index, cols=COLS_B):
        off, t = span(c)
        return hid.at[g, at(off, index, t // 4), cols]

    def gather1_b(g, c):
        share(("h1", g, c), ("h1", g), hid.at[g, rows_b(c), COLS_B], dev(dx=1))

    def gather1_a(g, c):
        for i, dy in ((0, 1), (1, -1)):
            share(("g1", g, c, i), ("g1", g), block_a(g, c, y), dev(dy=dy))

    def gather2_b(g, c):
        off, t = span(c)
        arrived(("h1", g, c), hid.at[g, at(off, y * 2 + xp, t // 8), COLS_B])
        for i, dy in ((0, 1), (1, -1)):
            share(("h2", g, c, i), ("h2", g), block_b(g, c, y), dev(dy=dy))

    def gather2_a(g, c):
        for i, block, dy in ((0, ym, 1), (1, yp, -1)):
            arrived(("g1", g, c, i), block_a(g, c, block))
            share(("g2", g, c), ("g2", g), block_a(g, c, block, pl.ds(i * HA, HA)), dev(dy=dy))

    def gather3_b(g, c):
        for i, block, dy in ((0, ym, 1), (1, yp, -1)):
            arrived(("h2", g, c, i), block_b(g, c, block))
            share(("h3", g, c), ("h3", g), block_b(g, c, block, pl.ds(CA + i * HB, HB)), dev(dy=dy))

    def gather3_a(g, c):
        off, t = span(c)
        arrived(("g2", g, c), block_a(g, c, y2))
        share(("g3", g, c), ("g3", g), hid.at[g, at(off, xl, t // 2), COLS_A], dev(dx=1))

    def gathered(g, c):
        off, t = span(c)
        arrived(("g3", g, c), hid.at[g, at(off, xp, t // 2), COLS_A])
        arrived(("h3", g, c), block_b(g, c, y2))

    ready = set()

    def all_gathered(g, chunks):
        for c in chunks:
            if (g, c) not in ready:
                ready.add((g, c))
                gathered(g, c)

    def back_product(c):
        all_gathered(0, (c,))
        off, t = span(c)
        s0, s1 = CHUNKS[c]
        out = lax.dot_general(
            hid[0, off:off + t, :], w_in[...], (((1,), (1,)), ((), ())),
            preferred_element_type=F32,
        )
        for slot in range(s0, s1):
            base = (slot - s0) * 128
            gk[slot] = out[base:base + 64]
            gs[slot] = out[base + 64:base + 128].astype(BF16)
        send(("n", c), ("n",), gs.at[pl.ds(s0, s1 - s0)], gr.at[pl.ds(s0, s1 - s0)], dev(dk=1))

    def scatter_x(c):
        s0, s1 = CHUNKS[c]
        arrived(("n", c), gr.at[pl.ds(s0, s1 - s0)])
        for slot in range(s0, s1):
            total = gk[slot] + gr[slot].astype(F32)
            gk[slot, 0:32] = total[0:32]
            xs[slot] = total[32:64].astype(BF16)
        send(("x", c), ("x",), xs.at[pl.ds(s0, s1 - s0)], xr.at[pl.ds(s0, s1 - s0)], dev(dh=1))

    def scatter_z(c):
        s0, s1 = CHUNKS[c]
        arrived(("x", c), xr.at[pl.ds(s0, s1 - s0)])
        for slot in range(s0, s1):
            total = gk[slot, 0:32] + xr[slot].astype(F32)
            if slot == 0:
                gk[0, 0:32] = total
            else:
                zs[slot] = total.astype(BF16)
                send(("s",), ("s",), zs.at[slot], zr.at[slot], dev(dz=DELTA[slot]))

    scale = float(TOKENS) ** (-0.5)
    tiles = [(i * 256, (i + 1) * 256) for i in range(3)]

    def outer(left, right):
        return lax.dot_general(
            left, right, (((0,), (0,)), ((), ())), preferred_element_type=F32
        )

    def flat(a, s0=0, s1=8):
        return gath[a, s0:s1].reshape((s1 - s0) * 128, BLK)

    def grad_in(n):
        all_gathered(0, range(LAST + 1))
        i, j = tiles[n]
        gwi[i:j, :] = (outer(flat(1)[:, i:j], hid[0]) * scale).astype(BF16)
        if n == 0:
            gb[...] = (jnp.sum(hid[0].astype(F32), 0, keepdims=True) * scale).reshape(BLK)

    def total_back():
        total = gk[0, 0:32]
        arrived(("s",), zr.at[pl.ds(1, 7)])
        for slot in range(1, 8):
            total = total + zr[slot].astype(F32)
        scaled = total * gain[...]
        ft[0] = pair(
            jnp.sum(scaled, 1, keepdims=True), jnp.sum(scaled * centred, 1, keepdims=True)
        )
        all_row("ft", ft)
        return scaled

    def finish_input(scaled):
        first, cross = row_sum("ft", ft)
        gi[...] = (inv_std * (scaled - first - centred * cross)).astype(BF16)

    def rows_out(c, i, j):
        s0, s1 = CHUNKS[c]
        return outer(hid[1, s0 * 128:s1 * 128, i:j], flat(0, s0, s1))

    def partial_out(c):
        all_gathered(1, (c,))
        for i, j in tiles:
            acc[i:j, :] = acc[i:j, :] + rows_out(c, i, j) if c else rows_out(c, i, j)

    def last_out():
        all_gathered(1, (LAST,))
        for i, j in tiles:
            gwo[i:j, :] = ((acc[i:j, :] + rows_out(LAST, i, j)) * scale).astype(BF16)

    own(0)
    all_row("st", st)
    mean_x, second = row_sum("st", st)
    inv_std = lax.rsqrt(second - mean_x * mean_x + EPS)
    centred = (values - mean_x) * inv_std
    loads[2].wait()
    gath[1, 0, 0, 0:32] = (centred * gain[...]).astype(BF16)
    own(1)
    other(0)
    loads[4].wait()
    product(0, 0)
    hop(0, 0, 1)
    other(1)
    loads[5].wait()
    product(1, 0)
    hop(0, 1, 1)
    hop(1, 0, 1)
    reduce2_a(0, 0)
    reduce2_b(0, 0)
    product(0, 1)
    hop(1, 1, 1)
    reduce2_b(1, 0)
    hop(0, 0, 2)
    reduce3_a(0, 0)
    reduce2_a(1, 0)
    product(1, 1)
    hop(0, 1, 2)
    reduce2_b(0, 1)
    hop(1, 0, 2)
    reduce2_a(0, 1)
    product(0, 2)
    reduce3_b(1, 0)
    hop(1, 1, 2)
    reduce3_a(1, 0)
    reduce2_b(1, 1)
    product(1, 2)
    hop(0, 0, 3)
    reduce3_a(0, 1)
    hop(0, 1, 3)
    reduce2_a(1, 1)
    hop(1, 0, 3)
    reduce3_b(0, 1)
    reduce3_b(0, 0)
    reduce2_b(0, 2)
    hop(1, 1, 3)
    product(0, 3)
    reduce2_a(0, 2)
    reduce2_a(1, 2)
    hop(0, 0, 4)
    reduce2_b(1, 2)
    hop(0, 1, 4)
    product(1, 3)
    reduce3_b(1, 1)
    reduce3_a(1, 1)
    hop(1, 1, 4)
    product(0, 4)
    reduce2_b(0, 3)
    reduce3_a(1, 2)
    hop(1, 0, 4)
    reduce3_b(0, 2)
    loads[3].wait()
    elementwise_a(0)
    reduce3_a(0, 2)
    product(1, 4)
    reduce3_b(1, 2)
    reduce2_b(1, 3)
    reduce2_a(0, 3)
    reduce2_a(1, 3)
    elementwise_b(1)
    gather1_a(0, 0)
    reduce2_b(0, 4)
    gather1_b(0, 1)
    reduce3_b(0, 3)
    reduce2_a(0, 4)
    elementwise_a(2)
    elementwise_b(0)
    gather1_b(0, 0)
    reduce2_b(1, 4)
    elementwise_a(1)
    reduce2_a(1, 4)
    gather1_a(0, 2)
    elementwise_b(2)
    gather1_a(0, 1)
    gather1_b(0, 2)
    reduce3_b(1, 3)
    gather1_b(1, 0)
    reduce3_a(0, 3)
    reduce3_a(1, 3)
    gather1_b(1, 1)
    gather2_a(0, 0)
    gather2_b(0, 1)
    reduce3_b(0, 4)
    reduce3_a(0, 4)
    reduce3_a(1, 4)
    reduce3_b(1, 4)
    gather2_a(0, 1)
    gather2_a(0, 2)
    elementwise_b(3)
    gather1_b(0, 3)
    elementwise_a(3)
    gather1_a(0, 3)
    gather3_a(0, 0)
    gather1_b(1, 2)
    gather2_b(0, 2)
    gather3_b(0, 1)
    elementwise_b(4)
    elementwise_a(4)
    gather1_b(0, 4)
    gather1_a(0, 4)
    gather3_a(0, 1)
    gather3_a(0, 2)
    gather2_a(0, 3)
    gather2_b(0, 3)
    gather3_b(0, 2)
    gather2_a(0, 4)
    gather2_b(0, 4)
    gather2_b(0, 0)
    gather3_a(0, 3)
    back_product(1)
    gather3_b(0, 3)
    gather1_a(1, 1)
    gather1_a(1, 3)
    gather3_a(0, 4)
    back_product(2)
    scatter_x(1)
    gather3_b(0, 4)
    gather1_a(1, 0)
    scatter_x(2)
    gather1_b(1, 4)
    gather3_b(0, 0)
    gather2_b(1, 0)
    back_product(3)
    gather1_b(1, 3)
    gather2_a(1, 1)
    back_product(4)
    gather1_a(1, 2)
    gather2_a(1, 0)
    gather2_a(1, 3)
    gather2_b(1, 2)
    scatter_x(4)
    scatter_z(1)
    scatter_x(3)
    gather1_a(1, 4)
    back_product(0)
    scatter_z(2)
    gather2_b(1, 4)
    gather2_b(1, 1)
    grad_in(2)
    gather3_a(1, 1)
    grad_in(0)
    gather3_a(1, 0)
    gather2_a(1, 2)
    gather3_b(1, 0)
    scatter_z(4)
    gather3_a(1, 3)
    gather2_a(1, 4)
    gather2_b(1, 3)
    scatter_x(0)
    scatter_z(3)
    gather3_b(1, 1)
    partial_out(0)
    gather3_a(1, 2)
    gather3_b(1, 2)
    gather3_b(1, 3)
    gather3_b(1, 4)
    scatter_z(0)
    gather3_a(1, 4)
    grad_in(1)
    partial_out(1)
    scaled = total_back()
    partial_out(2)
    partial_out(3)
    last_out()
    finish_input(scaled)

    for a in (0, 1):
        departed(("z", a), gath.at[a, pl.ds(0, 7), 0])
        departed(("k", a), gath.at[a, pl.ds(0, 7), 0])
        departed(("o", a), w_in.at[pl.ds(0, 96)])
        departed(("p", a), part.at[a, :, pl.ds(0, 256)])
        departed(("b", a), part.at[a, :, pl.ds(0, 256)])
        departed(("af", a), sa.at[a, pl.ds(0, 128)])
        departed(("a3", a), rbx.at[a])
        departed(("b3", a), rbx.at[a])
        departed(("g1", a), rbx.at[a])
        departed(("h1", a), rbx.at[a])
        departed(("h2", a), hid.at[a, :, pl.ds(0, 256)])
        departed(("g2", a), sa.at[a, pl.ds(0, 128)])
        departed(("g3", a), sa.at[a])
        departed(("h3", a), sb.at[a])
    departed(("n",), gs)
    departed(("x",), xs)
    departed(("s",), zs.at[pl.ds(1, 7)])
    departed(("st",), st.at[pl.ds(1, 7)])
    departed(("ft",), ft.at[pl.ds(1, 7)])


def deliver(*refs):
    sources, targets, sem = refs[:4], refs[4:8], refs[8]
    copies = [
        pltpu.make_async_copy(src, dst, sem.at[i])
        for i, (src, dst) in enumerate(zip(sources, targets))
    ]
    for copy in copies:
        copy.start()
    for copy in copies:
        copy.wait()


def local(inputs, gain, w_in, bias, w_out, cotangent):
    vmem = pl.BlockSpec(memory_space=pltpu.VMEM)
    anywhere = pl.BlockSpec(memory_space=pl.ANY)
    shapes = (
        jax.ShapeDtypeStruct((32, BLK), BF16),
        jax.ShapeDtypeStruct((BLK, BLK), BF16),
        jax.ShapeDtypeStruct((BLK,), F32),
        jax.ShapeDtypeStruct((BLK, BLK), BF16),
    )
    results = pl.pallas_call(
        kernel,
        out_shape=tuple(pltpu.VMEM(x.shape, x.dtype) for x in shapes),
        in_specs=[anywhere] * 6,
        out_specs=[vmem] * 4,
        scratch_shapes=[
            pltpu.VMEM((32, BLK), BF16),
            pltpu.VMEM((1, BLK), F32),
            pltpu.VMEM((BLK, BLK), BF16),
            pltpu.VMEM((1, BLK), F32),
            pltpu.VMEM((BLK, BLK), BF16),
            pltpu.VMEM((2, 8, 2, 64, BLK), BF16),
            pltpu.VMEM((2, TOKENS, BLK), BF16),
            pltpu.VMEM((2, TOKENS // 2, CA), BF16),
            pltpu.VMEM((2, TOKENS // 2, CA), BF16),
            pltpu.VMEM((2, 2, TOKENS // 8, HA), BF16),
            pltpu.VMEM((2, 2, TOKENS // 8, CA), BF16),
            pltpu.VMEM((2, 2, TOKENS // 4, HB), BF16),
            pltpu.VMEM((2, 2, TOKENS // 4, CB), BF16),
            pltpu.VMEM((2, TOKENS // 4, CB), BF16),
            pltpu.VMEM((2, TOKENS // 8, CB), BF16),
            pltpu.VMEM((2, TOKENS, BLK), BF16),
            pltpu.VMEM((8, 64, BLK), F32),
            pltpu.VMEM((8, 64, BLK), BF16),
            pltpu.VMEM((8, 64, BLK), BF16),
            pltpu.VMEM((8, 32, BLK), BF16),
            pltpu.VMEM((8, 32, BLK), BF16),
            pltpu.VMEM((8, 32, BLK), BF16),
            pltpu.VMEM((8, 32, BLK), BF16),
            pltpu.VMEM((BLK, BLK), F32),
            pltpu.VMEM((8, 8, 128), F32),
            pltpu.VMEM((8, 8, 128), F32),
            pltpu.SemaphoreType.DMA((6,)),
            pltpu.SemaphoreType.DMA((N_SEND,)),
            pltpu.SemaphoreType.DMA((N_RECV,)),
        ],
        compiler_params=pltpu.CompilerParams(
            collective_id=0, has_side_effects=True, vmem_limit_bytes=56 * 2**20
        ),
        name="mlp_backward",
    )(inputs, gain, w_in, bias, w_out, cotangent)
    return pl.pallas_call(
        deliver,
        out_shape=shapes,
        in_specs=[vmem] * 4,
        out_specs=[anywhere] * 4,
        scratch_shapes=[pltpu.SemaphoreType.DMA((4,))],
        compiler_params=pltpu.CompilerParams(vmem_limit_bytes=4 * 2**20),
        name="deliver",
    )(*results)


def solution(mesh):
    in_specs = (
        P("col", "row"),
        P("row"),
        P("row", "col"),
        P("col"),
        P("col", "row"),
        P("col", "row"),
    )
    out_specs = (P("col", "row"), P("row", "col"), P("col"), P("col", "row"))
    return jax.shard_map(local, mesh=mesh, in_specs=in_specs, out_specs=out_specs, check_vma=False)
```

```python
import functools

import jax
import jax.numpy as jnp
from jax import lax
from jax.experimental import pallas as pl
from jax.experimental.pallas import tpu as pltpu
from jax.sharding import PartitionSpec as P

MESH = pl.DeviceIdType.MESH
F32, BF16 = jnp.float32, jnp.bfloat16
D = 6144
EPS = 1e-06
TOKENS, BLK = 1024, 768
CA = 256
CB = BLK - CA
HA, HB = CA // 2, CB // 2
COLS_A, COLS_B = pl.ds(0, CA), pl.ds(CA, CB)
DELTA = (0, 1, -1, 2, -2, 3, -3, 4)
CHUNKS = ((0, 1), (1, 3), (3, 5), (5, 7), (7, 8))
LAST = len(CHUNKS) - 1
N_SEND, N_RECV = 33, 140


def normal_parts(pre_act):
    cumulative = 0.5 * (1.0 + lax.erf(pre_act * 0.7071067811865476))
    density = jnp.exp(-0.5 * pre_act * pre_act) * 0.3989422804014327
    return cumulative, density


def slot_of(delta):
    return DELTA.index(4 if delta in (4, -4) else delta)


def kernel(
    inp_hbm, gain_hbm, w_in_hbm, bias_hbm, w_out_hbm, cot_hbm, gi, gwi, gb, gwo,
    inp, gain, w_in, bias, w_out, gath, part, ra1, sa, raf, ra3, rbf, rb, sb, rbx, hid,
    gk, gs, gr, xs, xr, zs, zr, acc, st, ft, load_sem, send_sem, recv_sem,
):
    row, col = lax.axis_index("row"), lax.axis_index("col")
    y, xl = row // 2, row % 2
    xh, z, k = col // 16, (col // 2) % 8, col % 2

    def dev(dy=0, dx=0, dh=0, dz=0, dk=0):
        return (
            ((y + dy + 4) % 4) * 2 + (xl + dx) % 2,
            ((xh + dh) % 2) * 16 + ((z + dz + 8) % 8) * 2 + (k + dk) % 2,
        )

    xp, yp, ym, y2 = 1 - xl, (y + 1) % 4, (y + 3) % 4, (y + 2) % 4
    ROW_PEERS = [(dy, dx) for dy in range(4) for dx in range(2) if dy or dx]
    partners = [dev(dy=a, dx=b) for a, b in ROW_PEERS]
    partners += [dev(dz=1), dev(dz=-1), dev(dk=1), dev(dh=1), dev(dh=1, dk=1)]
    barrier = pltpu.get_barrier_semaphore()
    for partner in partners:
        pl.semaphore_signal(barrier, inc=1, device_id=partner, device_id_type=MESH)
    loads = [
        pltpu.make_async_copy(src, dst, load_sem.at[i])
        for i, (src, dst) in enumerate((
            (cot_hbm, gath.at[0, 0, 0, pl.ds(0, 32)]),
            (inp_hbm, inp),
            (gain_hbm, gain.at[0]),
            (bias_hbm, bias.at[0]),
            (w_out_hbm, w_out),
            (w_in_hbm, w_in),
        ))
    ]
    for load in loads:
        load.start()

    send_index, recv_index = {}, {}

    def slot_key(key):
        kind, c = key[0], key[2] if len(key) > 2 else 0
        if kind == "h1":
            return ("bf",) + key[1:]
        if kind == "g1":
            return ("a1" if key[3] == 0 else "af", key[1], c)
        if kind == "h2" and c > 0:
            return ("z", key[1], key[3], 7 if c == LAST else 2 * c)
        if kind in ("g2", "h3") and 0 < c < LAST:
            return ("z", key[1], 0 if kind == "g2" else 1, 2 * c - 1)
        return key

    def send(key, kind, src, dst, to):
        pltpu.make_async_remote_copy(
            src_ref=src, dst_ref=dst,
            send_sem=send_sem.at[send_index.setdefault(kind, len(send_index))],
            recv_sem=recv_sem.at[recv_index.setdefault(slot_key(key), len(recv_index))],
            device_id=to, device_id_type=MESH,
        ).start()

    def all_of(ref, kind, key):
        return pltpu.make_async_remote_copy(
            src_ref=ref, dst_ref=ref, send_sem=send_sem.at[send_index[kind]],
            recv_sem=recv_sem.at[recv_index[slot_key(key)]], device_id=dev(dk=1), device_id_type=MESH,
        )

    def arrived(key, ref):
        all_of(ref, ("st",), key).wait_recv()

    def departed(kind, ref):
        all_of(ref, kind, ("st",)).wait_send()

    lane = lax.broadcasted_iota(jnp.int32, (32, 128), 1)

    def pair(a, b):
        columns = jnp.where(lane < 64, a, b)
        return jnp.concatenate([columns, jnp.zeros((96, 128), F32)], 0).T[60:68]

    loads[0].wait()
    loads[1].wait()
    values = inp[...].astype(F32)
    st[0] = pair(
        jnp.sum(values, 1, keepdims=True), jnp.sum(values * values, 1, keepdims=True)
    )
    pl.semaphore_wait(barrier, len(partners))

    def all_row(tag, ref):
        for i, (dy, dx) in enumerate(ROW_PEERS):
            send((tag,), (tag,), ref.at[0], ref.at[i + 1], dev(dy=dy, dx=dx))

    def row_sum(tag, ref):
        arrived((tag,), ref.at[pl.ds(1, 7)])
        total = ref[0]
        for i in range(1, 8):
            total = total + ref[i]
        columns = jnp.concatenate([total, jnp.zeros((120, 128), F32)], 0).T
        return columns[0:32, 0:1] * (1.0 / D), columns[0:32, 4:5] * (1.0 / D)

    def unit(a, slot, u):
        return gath.at[a, slot, 0, pl.ds(u * 32, 32)]

    def pass_z(a, u, origin, slot, dz):
        send(("z", a, u, slot), ("z", a), unit(a, origin, u), unit(a, slot, u), dev(dz=dz))

    def z_first(a, u):
        pass_z(a, u, 0, 2, 1)
        pass_z(a, u, 0, 1, -1)

    def to_sibling(a, h, slot, u):
        mine = unit(a, slot, u)
        send(("k", a, min(h, LAST)), ("k", a), mine, gath.at[a, slot, 1, pl.ds(u * 32, 32)], dev(dk=1))

    def own(a):
        mine = unit(a, 0, 0)
        send(("h", a), ("o", a), mine, unit(a, 0, 1), dev(dh=1))
        z_first(a, 0)
        if a == 0:
            send(("k", a, 0), ("o", a), mine, gath.at[a, 0, 1, pl.ds(32, 32)], dev(dh=1, dk=1))
        send(("k", a, 0), ("o", a), mine, gath.at[a, 0, 1, pl.ds(0, 32)], dev(dk=1))

    def other(a):
        arrived(("h", a), unit(a, 0, 1))
        z_first(a, 1)
        if a == 1:
            send(("k", a, 0), ("o", a), unit(a, 0, 1), gath.at[a, 0, 1, pl.ds(32, 32)], dev(dk=1))

    def hop(a, u, h):
        if h == 4:
            arrived(("z", a, u, 7), unit(a, 7, u))
            to_sibling(a, h, 7, u)
            return
        for slot, dz in ((slot_of(-h), 1), (slot_of(h), -1)):
            arrived(("z", a, u, slot), unit(a, slot, u))
            to_sibling(a, h, slot, u)
            if h < 3 or u == (dz < 0):
                pass_z(a, u, slot, slot_of(-dz * (h + 1)), dz)

    def span(c):
        s0, s1 = CHUNKS[c]
        return s0 * 128, (s1 - s0) * 128

    def at(base, index, size):
        return pl.ds(pl.multiple_of(base + index * size, 16), size)

    def product(a, c):
        off, t = span(c)
        s0, s1 = CHUNKS[c]
        arrived(("k", a, c), gath.at[a, pl.ds(s0, s1 - s0), 1])
        rows = gath[a, s0:s1].reshape(t, BLK)
        if a == 0:
            out = lax.dot_general(
                rows, w_out[...], (((1,), (1,)), ((), ())), preferred_element_type=F32
            )
        else:
            out = jnp.dot(rows, w_in[...], preferred_element_type=F32)
        part[a, off:off + t, :] = out.astype(BF16)
        far = at(off, y2, t // 4)
        quarter = pl.ds(off // 4, t // 4)
        for i, dy in ((0, 1), (1, -1)):
            send(
                ("bf", a, c), ("p", a), part.at[a, far, pl.ds(CA + i * HB, HB)],
                rbf.at[a, i, quarter], dev(dy=dy),
            )
        send(
            ("a1", a, c), ("p", a), part.at[a, at(off, xp, t // 2), COLS_A],
            ra1.at[a, pl.ds(off // 2, t // 2)], dev(dx=1),
        )

    def merge(ref, a, rows, cols, other):
        ref[a, rows, cols] = (ref[a, rows, cols].astype(F32) + other.astype(F32)).astype(BF16)

    def reduce2_b(a, c):
        off, t = span(c)
        o4, t4 = off // 4, t // 4
        arrived(("bf", a, c), rbf.at[a, :, pl.ds(o4, t4)])
        for i, block, start, dy in ((0, yp, CA, 1), (1, ym, CA + HB, -1)):
            merge(part, a, at(off, block, t4), pl.ds(start, HB), rbf[a, i, o4:o4 + t4])
            send(
                ("b", a, c), ("b", a), part.at[a, at(off, block, t4), COLS_B],
                rb.at[a, i, pl.ds(o4, t4)], dev(dy=dy),
            )

    def reduce2_a(a, c):
        off, t = span(c)
        o2, o8, t2, t8 = off // 2, off // 8, t // 2, t // 8
        arrived(("a1", a, c), ra1.at[a, pl.ds(o2, t2)])
        total = part[a, at(off, xl, t2), COLS_A].astype(F32) + ra1[a, o2:o2 + t2].astype(F32)
        sa[a, o2:o2 + t2] = total.astype(BF16)
        for i, dy in ((0, 1), (1, -1)):
            send(
                ("af", a, c), ("af", a), sa.at[a, at(o2, y2, t8), pl.ds(i * HA, HA)],
                raf.at[a, i, pl.ds(o8, t8)], dev(dy=dy),
            )

    def reduce3_a(a, c):
        off, t = span(c)
        o2, o8, t8 = off // 2, off // 8, t // 8
        arrived(("af", a, c), raf.at[a, :, pl.ds(o8, t8)])
        for i, block, start, dy in ((0, yp, 0, 1), (1, ym, HA, -1)):
            merge(sa, a, at(o2, block, t8), pl.ds(start, HA), raf[a, i, o8:o8 + t8])
            send(
                ("a3", a, c), ("a3", a), sa.at[a, at(o2, block, t8)],
                ra3.at[a, i, pl.ds(o8, t8)], dev(dy=dy),
            )

    def reduce3_b(a, c):
        off, t = span(c)
        o4, o8, t4, t8 = off // 4, off // 8, t // 4, t // 8
        arrived(("b", a, c), rb.at[a, :, pl.ds(o4, t4)])
        total = part[a, at(off, y, t4), COLS_B].astype(F32)
        for i in (0, 1):
            total = total + rb[a, i, o4:o4 + t4].astype(F32)
        sb[a, o4:o4 + t4] = total.astype(BF16)
        send(
            ("b3", a, c), ("b3", a), sb.at[a, at(o4, xp, t8)], rbx.at[a, pl.ds(o8, t8)],
            dev(dx=1),
        )

    def rows_a(c):
        off, t = span(c)
        return at(off, xl * 4 + y, t // 8)

    def rows_b(c):
        off, t = span(c)
        return at(off, y * 2 + xl, t // 8)

    def finish(rows, cols, bias_part, totals):
        pre_act = totals[1] + bias_part
        cumulative, density = normal_parts(pre_act)
        hid[0, rows, cols] = (totals[0] * (cumulative + pre_act * density)).astype(BF16)
        hid[1, rows, cols] = (pre_act * cumulative).astype(BF16)

    def elementwise_a(c):
        off, t = span(c)
        o2, o8, t8 = off // 2, off // 8, t // 8
        totals = []
        for a in (0, 1):
            arrived(("a3", a, c), ra3.at[a, :, pl.ds(o8, t8)])
            total = sa[a, at(o2, y, t8)].astype(F32)
            for i in (0, 1):
                total = total + ra3[a, i, o8:o8 + t8].astype(F32)
            totals.append(total)
        finish(rows_a(c), COLS_A, bias[:, 0:CA], totals)

    def elementwise_b(c):
        off, t = span(c)
        o4, o8, t8 = off // 4, off // 8, t // 8
        totals = []
        for a in (0, 1):
            arrived(("b3", a, c), rbx.at[a, pl.ds(o8, t8)])
            totals.append(sb[a, at(o4, xl, t8)].astype(F32) + rbx[a, o8:o8 + t8].astype(F32))
        finish(rows_b(c), COLS_B, bias[:, CA:BLK], totals)

    def share(key, kind, ref, to):
        send(key, kind, ref, ref, to)

    def block_a(g, c, index, cols=COLS_A):
        off, t = span(c)
        return hid.at[g, at(off, xl * 4 + index, t // 8), cols]

    def block_b(g, c, index, cols=COLS_B):
        off, t = span(c)
        return hid.at[g, at(off, index, t // 4), cols]

    def gather1_b(g, c):
        share(("h1", g, c), ("h1", g), hid.at[g, rows_b(c), COLS_B], dev(dx=1))

    def gather1_a(g, c):
        for i, dy in ((0, 1), (1, -1)):
            share(("g1", g, c, i), ("g1", g), block_a(g, c, y), dev(dy=dy))

    def gather2_b(g, c):
        off, t = span(c)
        arrived(("h1", g, c), hid.at[g, at(off, y * 2 + xp, t // 8), COLS_B])
        for i, dy in ((0, 1), (1, -1)):
            share(("h2", g, c, i), ("h2", g), block_b(g, c, y), dev(dy=dy))

    def gather2_a(g, c):
        for i, block, dy in ((0, ym, 1), (1, yp, -1)):
            arrived(("g1", g, c, i), block_a(g, c, block))
            share(("g2", g, c), ("g2", g), block_a(g, c, block, pl.ds(i * HA, HA)), dev(dy=dy))

    def gather3_b(g, c):
        for i, block, dy in ((0, ym, 1), (1, yp, -1)):
            arrived(("h2", g, c, i), block_b(g, c, block))
            share(("h3", g, c), ("h3", g), block_b(g, c, block, pl.ds(CA + i * HB, HB)), dev(dy=dy))

    def gather3_a(g, c):
        off, t = span(c)
        arrived(("g2", g, c), block_a(g, c, y2))
        share(("g3", g, c), ("g3", g), hid.at[g, at(off, xl, t // 2), COLS_A], dev(dx=1))

    def gathered(g, c):
        off, t = span(c)
        arrived(("g3", g, c), hid.at[g, at(off, xp, t // 2), COLS_A])
        arrived(("h3", g, c), block_b(g, c, y2))

    ready = set()

    def all_gathered(g, chunks):
        for c in chunks:
            if (g, c) not in ready:
                ready.add((g, c))
                gathered(g, c)

    def back_product(c):
        all_gathered(0, (c,))
        off, t = span(c)
        s0, s1 = CHUNKS[c]
        out = lax.dot_general(
            hid[0, off:off + t, :], w_in[...], (((1,), (1,)), ((), ())),
            preferred_element_type=F32,
        )
        for slot in range(s0, s1):
            base = (slot - s0) * 128
            gk[slot] = out[base:base + 64]
            gs[slot] = out[base + 64:base + 128].astype(BF16)
        send(("n", c), ("n",), gs.at[pl.ds(s0, s1 - s0)], gr.at[pl.ds(s0, s1 - s0)], dev(dk=1))

    def scatter_x(c):
        s0, s1 = CHUNKS[c]
        arrived(("n", c), gr.at[pl.ds(s0, s1 - s0)])
        for slot in range(s0, s1):
            total = gk[slot] + gr[slot].astype(F32)
            gk[slot, 0:32] = total[0:32]
            xs[slot] = total[32:64].astype(BF16)
        send(("x", c), ("x",), xs.at[pl.ds(s0, s1 - s0)], xr.at[pl.ds(s0, s1 - s0)], dev(dh=1))

    def scatter_z(c):
        s0, s1 = CHUNKS[c]
        arrived(("x", c), xr.at[pl.ds(s0, s1 - s0)])
        for slot in range(s0, s1):
            total = gk[slot, 0:32] + xr[slot].astype(F32)
            if slot == 0:
                gk[0, 0:32] = total
            else:
                zs[slot] = total.astype(BF16)
                send(("s",), ("s",), zs.at[slot], zr.at[slot], dev(dz=DELTA[slot]))

    scale = float(TOKENS) ** (-0.5)
    tiles = [(i * 256, (i + 1) * 256) for i in range(3)]

    def outer(left, right):
        return lax.dot_general(
            left, right, (((0,), (0,)), ((), ())), preferred_element_type=F32
        )

    def flat(a, s0=0, s1=8):
        return gath[a, s0:s1].reshape((s1 - s0) * 128, BLK)

    def grad_in(n):
        all_gathered(0, range(LAST + 1))
        i, j = tiles[n]
        gwi[i:j, :] = (outer(flat(1)[:, i:j], hid[0]) * scale).astype(BF16)
        if n == 0:
            gb[...] = (jnp.sum(hid[0].astype(F32), 0, keepdims=True) * scale).reshape(BLK)

    def total_back():
        total = gk[0, 0:32]
        arrived(("s",), zr.at[pl.ds(1, 7)])
        for slot in range(1, 8):
            total = total + zr[slot].astype(F32)
        scaled = total * gain[...]
        ft[0] = pair(
            jnp.sum(scaled, 1, keepdims=True), jnp.sum(scaled * centred, 1, keepdims=True)
        )
        all_row("ft", ft)
        return scaled

    def finish_input(scaled):
        first, cross = row_sum("ft", ft)
        gi[...] = (inv_std * (scaled - first - centred * cross)).astype(BF16)

    def rows_out(c, i, j):
        s0, s1 = CHUNKS[c]
        return outer(hid[1, s0 * 128:s1 * 128, i:j], flat(0, s0, s1))

    def partial_out(c):
        all_gathered(1, (c,))
        for i, j in tiles:
            acc[i:j, :] = acc[i:j, :] + rows_out(c, i, j) if c else rows_out(c, i, j)

    def last_out():
        all_gathered(1, (LAST,))
        for i, j in tiles:
            gwo[i:j, :] = ((acc[i:j, :] + rows_out(LAST, i, j)) * scale).astype(BF16)

    own(0)
    all_row("st", st)
    mean_x, second = row_sum("st", st)
    inv_std = lax.rsqrt(second - mean_x * mean_x + EPS)
    centred = (values - mean_x) * inv_std
    loads[2].wait()
    gath[1, 0, 0, 0:32] = (centred * gain[...]).astype(BF16)
    own(1)
    other(0)
    loads[4].wait()
    product(0, 0)
    hop(0, 0, 1)
    other(1)
    loads[5].wait()
    product(1, 0)
    hop(0, 1, 1)
    hop(1, 0, 1)
    reduce2_a(0, 0)
    reduce2_b(0, 0)
    product(0, 1)
    hop(1, 1, 1)
    reduce2_b(1, 0)
    hop(0, 0, 2)
    reduce3_a(0, 0)
    reduce2_a(1, 0)
    product(1, 1)
    hop(0, 1, 2)
    reduce2_b(0, 1)
    hop(1, 0, 2)
    reduce2_a(0, 1)
    product(0, 2)
    reduce3_b(1, 0)
    hop(1, 1, 2)
    reduce3_a(1, 0)
    reduce2_b(1, 1)
    product(1, 2)
    hop(0, 0, 3)
    reduce3_a(0, 1)
    hop(0, 1, 3)
    reduce2_a(1, 1)
    hop(1, 0, 3)
    reduce3_b(0, 1)
    reduce3_b(0, 0)
    reduce2_b(0, 2)
    hop(1, 1, 3)
    product(0, 3)
    reduce2_a(0, 2)
    reduce2_a(1, 2)
    hop(0, 0, 4)
    reduce2_b(1, 2)
    hop(0, 1, 4)
    product(1, 3)
    reduce3_b(1, 1)
    reduce3_a(1, 1)
    hop(1, 1, 4)
    product(0, 4)
    reduce2_b(0, 3)
    reduce3_a(1, 2)
    hop(1, 0, 4)
    reduce3_b(0, 2)
    loads[3].wait()
    elementwise_a(0)
    reduce3_a(0, 2)
    product(1, 4)
    reduce3_b(1, 2)
    reduce2_b(1, 3)
    reduce2_a(0, 3)
    reduce2_a(1, 3)
    elementwise_b(1)
    gather1_a(0, 0)
    reduce2_b(0, 4)
    gather1_b(0, 1)
    reduce3_b(0, 3)
    reduce2_a(0, 4)
    elementwise_a(2)
    elementwise_b(0)
    gather1_b(0, 0)
    reduce2_b(1, 4)
    elementwise_a(1)
    reduce2_a(1, 4)
    gather1_a(0, 2)
    elementwise_b(2)
    gather1_a(0, 1)
    gather1_b(0, 2)
    reduce3_b(1, 3)
    gather1_b(1, 0)
    reduce3_a(0, 3)
    reduce3_a(1, 3)
    gather1_b(1, 1)
    gather2_a(0, 0)
    gather2_b(0, 1)
    reduce3_b(0, 4)
    reduce3_a(0, 4)
    reduce3_a(1, 4)
    reduce3_b(1, 4)
    gather2_a(0, 1)
    gather2_a(0, 2)
    elementwise_b(3)
    gather1_b(0, 3)
    elementwise_a(3)
    gather1_a(0, 3)
    gather3_a(0, 0)
    gather1_b(1, 2)
    gather2_b(0, 2)
    gather3_b(0, 1)
    elementwise_b(4)
    elementwise_a(4)
    gather1_b(0, 4)
    gather1_a(0, 4)
    gather3_a(0, 1)
    gather3_a(0, 2)
    gather2_a(0, 3)
    gather2_b(0, 3)
    gather3_b(0, 2)
    gather2_a(0, 4)
    gather2_b(0, 4)
    gather2_b(0, 0)
    gather3_a(0, 3)
    back_product(1)
    gather3_b(0, 3)
    gather1_a(1, 1)
    gather1_a(1, 3)
    gather3_a(0, 4)
    back_product(2)
    scatter_x(1)
    gather3_b(0, 4)
    gather1_a(1, 0)
    scatter_x(2)
    gather1_b(1, 4)
    gather3_b(0, 0)
    gather2_b(1, 0)
    back_product(3)
    gather1_b(1, 3)
    gather2_a(1, 1)
    back_product(4)
    gather1_a(1, 2)
    gather2_a(1, 0)
    gather2_a(1, 3)
    gather2_b(1, 2)
    scatter_x(4)
    scatter_z(1)
    scatter_x(3)
    gather1_a(1, 4)
    back_product(0)
    scatter_z(2)
    gather2_b(1, 4)
    gather2_b(1, 1)
    grad_in(2)
    gather3_a(1, 1)
    grad_in(0)
    gather3_a(1, 0)
    gather2_a(1, 2)
    gather3_b(1, 0)
    scatter_z(4)
    gather3_a(1, 3)
    gather2_a(1, 4)
    gather2_b(1, 3)
    scatter_x(0)
    scatter_z(3)
    gather3_b(1, 1)
    partial_out(0)
    gather3_a(1, 2)
    gather3_b(1, 2)
    gather3_b(1, 3)
    gather3_b(1, 4)
    scatter_z(0)
    gather3_a(1, 4)
    grad_in(1)
    partial_out(1)
    scaled = total_back()
    partial_out(2)
    partial_out(3)
    last_out()
    finish_input(scaled)

    for a in (0, 1):
        departed(("z", a), gath.at[a, pl.ds(0, 7), 0])
        departed(("k", a), gath.at[a, pl.ds(0, 7), 0])
        departed(("o", a), w_in.at[pl.ds(0, 96)])
        departed(("p", a), part.at[a, :, pl.ds(0, 256)])
        departed(("b", a), part.at[a, :, pl.ds(0, 256)])
        departed(("af", a), sa.at[a, pl.ds(0, 128)])
        departed(("a3", a), rbx.at[a])
        departed(("b3", a), rbx.at[a])
        departed(("g1", a), rbx.at[a])
        departed(("h1", a), rbx.at[a])
        departed(("h2", a), hid.at[a, :, pl.ds(0, 256)])
        departed(("g2", a), sa.at[a, pl.ds(0, 128)])
        departed(("g3", a), sa.at[a])
        departed(("h3", a), sb.at[a])
    departed(("n",), gs)
    departed(("x",), xs)
    departed(("s",), zs.at[pl.ds(1, 7)])
    departed(("st",), st.at[pl.ds(1, 7)])
    departed(("ft",), ft.at[pl.ds(1, 7)])


def deliver(*refs):
    sources, targets, sem = refs[:4], refs[4:8], refs[8]
    copies = [
        pltpu.make_async_copy(src, dst, sem.at[i])
        for i, (src, dst) in enumerate(zip(sources, targets))
    ]
    for copy in copies:
        copy.start()
    for copy in copies:
        copy.wait()


def local(inputs, gain, w_in, bias, w_out, cotangent):
    vmem = pl.BlockSpec(memory_space=pltpu.VMEM)
    anywhere = pl.BlockSpec(memory_space=pl.ANY)
    shapes = (
        jax.ShapeDtypeStruct((32, BLK), BF16),
        jax.ShapeDtypeStruct((BLK, BLK), BF16),
        jax.ShapeDtypeStruct((BLK,), F32),
        jax.ShapeDtypeStruct((BLK, BLK), BF16),
    )
    results = pl.pallas_call(
        kernel,
        out_shape=tuple(pltpu.VMEM(x.shape, x.dtype) for x in shapes),
        in_specs=[anywhere] * 6,
        out_specs=[vmem] * 4,
        scratch_shapes=[
            pltpu.VMEM((32, BLK), BF16),
            pltpu.VMEM((1, BLK), F32),
            pltpu.VMEM((BLK, BLK), BF16),
            pltpu.VMEM((1, BLK), F32),
            pltpu.VMEM((BLK, BLK), BF16),
            pltpu.VMEM((2, 8, 2, 64, BLK), BF16),
            pltpu.VMEM((2, TOKENS, BLK), BF16),
            pltpu.VMEM((2, TOKENS // 2, CA), BF16),
            pltpu.VMEM((2, TOKENS // 2, CA), BF16),
            pltpu.VMEM((2, 2, TOKENS // 8, HA), BF16),
            pltpu.VMEM((2, 2, TOKENS // 8, CA), BF16),
            pltpu.VMEM((2, 2, TOKENS // 4, HB), BF16),
            pltpu.VMEM((2, 2, TOKENS // 4, CB), BF16),
            pltpu.VMEM((2, TOKENS // 4, CB), BF16),
            pltpu.VMEM((2, TOKENS // 8, CB), BF16),
            pltpu.VMEM((2, TOKENS, BLK), BF16),
            pltpu.VMEM((8, 64, BLK), F32),
            pltpu.VMEM((8, 64, BLK), BF16),
            pltpu.VMEM((8, 64, BLK), BF16),
            pltpu.VMEM((8, 32, BLK), BF16),
            pltpu.VMEM((8, 32, BLK), BF16),
            pltpu.VMEM((8, 32, BLK), BF16),
            pltpu.VMEM((8, 32, BLK), BF16),
            pltpu.VMEM((BLK, BLK), F32),
            pltpu.VMEM((8, 8, 128), F32),
            pltpu.VMEM((8, 8, 128), F32),
            pltpu.SemaphoreType.DMA((6,)),
            pltpu.SemaphoreType.DMA((N_SEND,)),
            pltpu.SemaphoreType.DMA((N_RECV,)),
        ],
        compiler_params=pltpu.CompilerParams(
            collective_id=0, has_side_effects=True, vmem_limit_bytes=56 * 2**20
        ),
        name="mlp_backward",
    )(inputs, gain, w_in, bias, w_out, cotangent)
    return pl.pallas_call(
        deliver,
        out_shape=shapes,
        in_specs=[vmem] * 4,
        out_specs=[anywhere] * 4,
        scratch_shapes=[pltpu.SemaphoreType.DMA((4,))],
        compiler_params=pltpu.CompilerParams(vmem_limit_bytes=4 * 2**20),
        name="deliver",
    )(*results)


def solution(mesh):
    in_specs = (
        P("col", "row"),
        P("row"),
        P("row", "col"),
        P("col"),
        P("col", "row"),
        P("col", "row"),
    )
    out_specs = (P("col", "row"), P("row", "col"), P("col"), P("col", "row"))
    return jax.shard_map(local, mesh=mesh, in_specs=in_specs, out_specs=out_specs, check_vma=False)
```
